256 devices in a mesh: section: 32 (over z_hi, y, core), fsdp: 8 (over z_lo, x).
Axes of the slice: x: 4, y: 4, z: 8 (z_hi: 4, z_lo: 2; z = z_hi * 2 + z_lo), core: 2. Of those that a mesh axis runs over, the one named last changes fastest.
Arguments:
- handoff: bfloat16 [32, 8192, 640], P('section', 'fsdp'), may hold values from -6 to 6
- returning: bfloat16 [32, 8192, 640], P('section', 'fsdp'), may hold values from -6 to 6
- stashed_input: bfloat16 [32, 8192, 640], P('section', 'fsdp'), may hold values from -6 to 6
- skip_held: bfloat16 [32, 8192, 640], P('section', 'fsdp'), may hold values from -6 to 6
- timesteps_forward: int32 [32, 8], P('section', 'fsdp'), may hold values from 0 to 999
- timesteps_backward: int32 [32, 8], P('section', 'fsdp'), may hold values from 0 to 999
- section_level: int32 [32], P('section'), may hold values from 0 to 3
- level_embed: float32 [4, 256], replicated, may hold values from -6 to 6
- temporal_weight: bfloat16 [32, 1920, 640], P('section', 'fsdp'), may hold values from -0.125 to 0.125
- point_weight: bfloat16 [32, 640, 640], P('section', 'fsdp'), may hold values from -0.25 to 0.25
- film_weight: bfloat16 [32, 256, 1280], P('section', 'fsdp'), may hold values from -0.375 to 0.375
Outputs:
- handoff_next: bfloat16 [32, 8192, 640], P('section', 'fsdp')
- returning_next: bfloat16 [32, 8192, 640], P('section', 'fsdp')
- skip_next: bfloat16 [32, 8192, 640], P('section', 'fsdp')
- temporal_grad: float32 [32, 1920, 640], P('section', 'fsdp')
- pointwise_grad: float32 [32, 640, 640], P('section', 'fsdp')
- film_grad: float32 [32, 256, 1280], P('section', 'fsdp')
The draws below stay inside these ranges and needn't reach their ends.
All inputs are finite; a program needn't handle non-finite values.
Results may differ from the reference program's by a relative error of at most 0.025.
Values may be sent and summed in bfloat16 or wider, within the bound.
A program may use at most 128 MiB of HBM per device.

```python
import math
import jax
import jax.numpy as jnp
from jax import lax

CHANNELS = 640
EMBED = 256
FRAMES = 16
SAMP_DEV = 1
LEVELS = 4
SECTIONS = 32
SAMPLES = 8
ROWS = 8192
N_FSDP = 8


def with_ends(values, key, low, high):
    longest = values.shape.index(max(values.shape))
    spots = []
    for shift in (0, 1):
        where = [jax.random.randint(jax.random.fold_in(key, axis), (), 0, length) for axis, length in enumerate(values.shape)]
        where[longest] = (where[longest] + shift) % values.shape[longest]
        spots.append(tuple(where))
    return values.at[spots[0]].set(low).at[spots[1]].set(high)


def block_scale(own_key, shape, shards, least, largest):
    def one(axis_at, parts):
        draws = jax.random.uniform(jax.random.fold_in(jax.random.fold_in(own_key, 6), axis_at), (parts,), jnp.float32, least / len(shards), largest / len(shards))
        return jnp.repeat(jnp.exp(draws), shape[axis_at] // parts).reshape((-1,) + (1,) * (len(shape) - axis_at - 1))

    gain = one(*shards[0])
    for cut in shards[1:]:
        gain = gain * one(*cut)
    return gain


def bell_draw(own_key, shape, width, limit, cuts=(), held_as=jnp.bfloat16):
    entries = jax.random.normal(own_key, shape, jnp.float32) * width
    if len(cuts) > 0:
        entries = block_scale(own_key, shape, cuts, -0.22, 0.18) * entries
    return jnp.clip(entries, min=-limit, max=limit).astype(held_as)


def setup_inputs(seed: int = 0) -> dict:
    key_list = jax.random.split(jax.random.key(seed), 12)
    return {
        "handoff": bell_draw(key_list[0], (SECTIONS, ROWS, CHANNELS), 1.0, 6.0, ((0, 32), (1, 8))),
        "returning": bell_draw(key_list[1], (SECTIONS, ROWS, CHANNELS), 1.0, 6.0, ((0, 32), (1, 8))),
        "stashed_input": bell_draw(key_list[2], (SECTIONS, ROWS, CHANNELS), 1.0, 6.0, ((0, 32), (1, 8))),
        "skip_held": bell_draw(key_list[3], (SECTIONS, ROWS, CHANNELS), 1.0, 6.0, ((0, 32), (1, 8))),
        "timesteps_forward": with_ends(jax.random.randint(key_list[4], (SECTIONS, SAMPLES), 0, 1000), jax.random.fold_in(key_list[4], 1), 0, 999).astype(jnp.int32),
        "timesteps_backward": with_ends(jax.random.randint(key_list[5], (SECTIONS, SAMPLES), 0, 1000), jax.random.fold_in(key_list[5], 1), 0, 999).astype(jnp.int32),
        "section_level": with_ends(jax.random.randint(key_list[6], (SECTIONS,), 0, LEVELS), jax.random.fold_in(key_list[6], 1), 0, LEVELS - 1).astype(jnp.int32),
        "level_embed": bell_draw(key_list[7], (LEVELS, EMBED), 1.0, 6.0, (), jnp.float32),
        "temporal_weight": bell_draw(key_list[8], (SECTIONS, 3 * CHANNELS, CHANNELS), (3 * CHANNELS) ** -0.5, 0.125, ((0, 32), (1, 8))),
        "point_weight": bell_draw(key_list[9], (SECTIONS, CHANNELS, CHANNELS), CHANNELS ** -0.5, 0.25, ((0, 32), (1, 8))),
        "film_weight": bell_draw(key_list[10], (SECTIONS, EMBED, 2 * CHANNELS), EMBED ** -0.5, 0.375, ((0, 32), (1, 8))),
    }


def lookup_level(level_embed, level_index):
    onehot = (jnp.arange(LEVELS, dtype=jnp.int32) == level_index).astype(jnp.float32)
    return lax.optimization_barrier(jnp.sum(onehot[:, None] * level_embed, axis=0))

def time_hidden(timesteps, level_row):
    half_width = EMBED // 2
    frequency = jnp.exp(-math.log(10000.0) * jnp.arange(half_width, dtype=jnp.float32) / half_width)
    phases = timesteps.astype(jnp.float32)[:, None] * frequency[None, :]
    embedded = jnp.concatenate([jnp.sin(phases), jnp.cos(phases)], axis=-1) + level_row[None, :]
    return jax.nn.silu(embedded).astype(jnp.bfloat16)

def unet_block(block_input, hidden, temporal_weight, point_weight, film_weight):
    sample_count = hidden.shape[0]
    film = jnp.dot(hidden, film_weight, preferred_element_type=jnp.float32)
    film_scale = film[:, :CHANNELS][:, None, None, :]
    film_shift = film[:, CHANNELS:][:, None, None, :]
    grid = block_input.reshape(sample_count, FRAMES, -1, CHANNELS)
    mean_square = lax.optimization_barrier(jnp.mean(grid * grid, axis=-1, keepdims=True))
    normalized = grid * lax.rsqrt(mean_square + 1e-06)
    modulated = (normalized * (1.0 + film_scale) + film_shift).astype(jnp.bfloat16)
    blank = jnp.zeros_like(modulated[:, :1])
    earlier = jnp.concatenate([blank, modulated[:, :-1]], axis=1)
    later_frame = jnp.concatenate([modulated[:, 1:], blank], axis=1)
    stacked = jnp.concatenate([earlier, modulated, later_frame], axis=-1).reshape(-1, 3 * CHANNELS)
    temporal = jnp.dot(stacked, temporal_weight, preferred_element_type=jnp.float32)
    gated = jax.nn.silu(temporal).astype(jnp.bfloat16)
    return block_input + jnp.dot(gated, point_weight, preferred_element_type=jnp.float32)

def forward_section(operands, level_embed):
    block_input, timesteps, level_index, temporal_weight, point_weight, film_weight = operands
    hidden = time_hidden(timesteps, lookup_level(level_embed, level_index))
    return unet_block(block_input, hidden, temporal_weight, point_weight, film_weight).astype(jnp.bfloat16)

def backward_section(operands, level_embed):
    block_input, output_grad, timesteps, level_index, temporal_weight, point_weight, film_weight = operands
    level_row = lookup_level(level_embed, level_index)
    inputs_split = block_input.reshape(N_FSDP, -1, CHANNELS)
    grads_split = output_grad.reshape(N_FSDP, -1, CHANNELS)
    steps_split = timesteps.reshape(N_FSDP, SAMP_DEV)

    def shard_pull(shard):
        shard_input, shard_grad, shard_steps = shard
        hidden = time_hidden(shard_steps, level_row)

        def local_block(first, second, third, fourth):
            return unet_block(first, hidden, second, third, fourth)
        unused, pullback = jax.vjp(local_block, shard_input.astype(jnp.float32), temporal_weight, point_weight, film_weight)
        input_grad, grad_one, grad_two, grad_three = pullback(shard_grad)
        return (input_grad, grad_one.astype(jnp.float32), grad_two.astype(jnp.float32), grad_three.astype(jnp.float32))
    input_grad, grad_one, grad_two, grad_three = lax.map(shard_pull, (inputs_split, grads_split, steps_split))
    return (input_grad.reshape(-1, CHANNELS).astype(jnp.bfloat16), lax.optimization_barrier(jnp.sum(grad_one, axis=0)), lax.optimization_barrier(jnp.sum(grad_two, axis=0)), lax.optimization_barrier(jnp.sum(grad_three, axis=0)))

def reference(handoff, returning, stashed_input, skip_held, timesteps_forward, timesteps_backward, section_level, level_embed, temporal_weight, point_weight, film_weight):
    midpoint = SECTIONS // 2
    arrived = jnp.roll(handoff, 1, axis=0).astype(jnp.float32)
    going_back = jnp.roll(returning, -1, axis=0).astype(jnp.float32)
    held_rows = skip_held.astype(jnp.float32)

    def forward_map(operands):
        return forward_section(operands, level_embed)

    def backward_map(operands):
        return backward_section(operands, level_embed)
    encoder_out = lax.map(forward_map, (arrived[:midpoint], timesteps_forward[:midpoint], section_level[:midpoint], temporal_weight[:midpoint], point_weight[:midpoint], film_weight[:midpoint]))
    decoder_out = lax.map(forward_map, (arrived[midpoint:] + held_rows[midpoint:], timesteps_forward[midpoint:], section_level[midpoint:], temporal_weight[midpoint:], point_weight[midpoint:], film_weight[midpoint:]))
    handoff_next = jnp.concatenate([encoder_out, decoder_out], axis=0)
    decoder_back = lax.map(backward_map, (stashed_input[midpoint:], going_back[midpoint:], timesteps_backward[midpoint:], section_level[midpoint:], temporal_weight[midpoint:], point_weight[midpoint:], film_weight[midpoint:]))
    encoder_back = lax.map(backward_map, (stashed_input[:midpoint], going_back[:midpoint] + held_rows[:midpoint], timesteps_backward[:midpoint], section_level[:midpoint], temporal_weight[:midpoint], point_weight[:midpoint], film_weight[:midpoint]))
    returning_next = jnp.concatenate([encoder_back[0], decoder_back[0]], axis=0)
    skip_next = jnp.concatenate([decoder_back[0][::-1], encoder_out[::-1]], axis=0)
    temporal_grad = jnp.concatenate([encoder_back[1], decoder_back[1]], axis=0)
    pointwise_grad = jnp.concatenate([encoder_back[2], decoder_back[2]], axis=0)
    film_grad = jnp.concatenate([encoder_back[3], decoder_back[3]], axis=0)
    return (handoff_next, returning_next, skip_next, temporal_grad, pointwise_grad, film_grad)
```

```python
import math

import jax
import jax.numpy as jnp
from jax import lax
from jax.sharding import PartitionSpec as P

CHANNELS = 640
EMBED = 256
FRAMES = 16
LEVELS = 4


def passed_along(x, axis, by):
    length = lax.axis_size(axis)
    return lax.ppermute(x, axis, [(i, (i + by) % length) for i in range(length)])


def lookup_level(level_embed, level_index):
    onehot = (jnp.arange(LEVELS, dtype=jnp.int32) == level_index).astype(jnp.float32)
    return jnp.sum(onehot[:, None] * level_embed, axis=0)


def time_hidden(timesteps, level_row):
    half_width = EMBED // 2
    frequency = jnp.exp(-math.log(10000.0) * jnp.arange(half_width, dtype=jnp.float32) / half_width)
    phases = timesteps.astype(jnp.float32)[:, None] * frequency[None, :]
    embedded = jnp.concatenate([jnp.sin(phases), jnp.cos(phases)], axis=-1) + level_row[None, :]
    return jax.nn.silu(embedded).astype(jnp.bfloat16)


def unet_block(block_input, hidden, temporal_weight, point_weight, film_weight):
    sample_count = hidden.shape[0]
    film = jnp.dot(hidden, film_weight, preferred_element_type=jnp.float32)
    film_scale = film[:, :CHANNELS][:, None, None, :]
    film_shift = film[:, CHANNELS:][:, None, None, :]
    grid = block_input.reshape(sample_count, FRAMES, -1, CHANNELS)
    mean_square = jnp.mean(grid * grid, axis=-1, keepdims=True)
    normalized = grid * lax.rsqrt(mean_square + 1e-06)
    modulated = (normalized * (1.0 + film_scale) + film_shift).astype(jnp.bfloat16)
    blank = jnp.zeros_like(modulated[:, :1])
    earlier = jnp.concatenate([blank, modulated[:, :-1]], axis=1)
    later_frame = jnp.concatenate([modulated[:, 1:], blank], axis=1)
    stacked = jnp.concatenate([earlier, modulated, later_frame], axis=-1).reshape(-1, 3 * CHANNELS)
    temporal = jnp.dot(stacked, temporal_weight, preferred_element_type=jnp.float32)
    gated = jax.nn.silu(temporal).astype(jnp.bfloat16)
    return block_input + jnp.dot(gated, point_weight, preferred_element_type=jnp.float32)


def body(
    handoff,
    returning,
    stashed_input,
    skip_held,
    timesteps_forward,
    timesteps_backward,
    section_level,
    level_embed,
    temporal_weight,
    point_weight,
    film_weight,
):
    sections = lax.axis_size("section")
    midpoint = sections // 2
    encoder_side = lax.axis_index("section") < midpoint
    full_temporal, full_point, full_film = (
        lax.all_gather(temporal_weight, "fsdp", axis=1, tiled=True),
        lax.all_gather(point_weight, "fsdp", axis=1, tiled=True),
        lax.all_gather(film_weight, "fsdp", axis=1, tiled=True),
    )
    full_temporal, full_point, full_film = (full_temporal[0], full_point[0], full_film[0])
    arrived = passed_along(handoff, "section", 1)[0].astype(jnp.float32)
    going_back = passed_along(returning, "section", -1)[0].astype(jnp.float32)
    held_rows = skip_held[0].astype(jnp.float32)
    level_row = lookup_level(level_embed, section_level[0])
    hidden_forward = time_hidden(timesteps_forward[0], level_row)
    hidden_backward = time_hidden(timesteps_backward[0], level_row)
    stash_rows = stashed_input[0].astype(jnp.float32)

    def backward(output_grad):

        def local_block(first, second, third, fourth):
            return unet_block(first, hidden_backward, second, third, fourth)

        unused, pullback = jax.vjp(local_block, stash_rows, full_temporal, full_point, full_film)
        input_grad, grad_one, grad_two, grad_three = pullback(output_grad)
        return (
            input_grad.astype(jnp.bfloat16),
            (
                grad_one.astype(jnp.float32),
                grad_two.astype(jnp.float32),
                grad_three.astype(jnp.float32),
            ),
        )

    forward_input = arrived + jnp.where(encoder_side, 0.0, held_rows)
    backward_grad = going_back + jnp.where(encoder_side, held_rows, 0.0)
    section_out = unet_block(
        forward_input, hidden_forward, full_temporal, full_point, full_film
    ).astype(jnp.bfloat16)
    input_grad, weight_grads = backward(backward_grad)
    leaving = jnp.where(encoder_side, section_out, input_grad)
    skip_next = lax.ppermute(leaving, "section", [(i, sections - 1 - i) for i in range(sections)])
    temporal_grad, pointwise_grad, film_grad = (
        lax.psum_scatter(
            weight_grads[0][None].astype(jnp.bfloat16), "fsdp", scatter_dimension=1, tiled=True
        ).astype(jnp.float32),
        lax.psum_scatter(
            weight_grads[1][None].astype(jnp.bfloat16), "fsdp", scatter_dimension=1, tiled=True
        ).astype(jnp.float32),
        lax.psum_scatter(
            weight_grads[2][None].astype(jnp.bfloat16), "fsdp", scatter_dimension=1, tiled=True
        ).astype(jnp.float32),
    )
    return (
        section_out[None],
        input_grad[None],
        skip_next[None],
        temporal_grad,
        pointwise_grad,
        film_grad,
    )


def solution(mesh):
    in_specs = (
        P("section", "fsdp", None),
        P("section", "fsdp", None),
        P("section", "fsdp", None),
        P("section", "fsdp", None),
        P("section", "fsdp"),
        P("section", "fsdp"),
        P("section"),
        P(),
        P("section", "fsdp", None),
        P("section", "fsdp", None),
        P("section", "fsdp", None),
    )
    out_specs = (
        P("section", "fsdp", None),
        P("section", "fsdp", None),
        P("section", "fsdp", None),
        P("section", "fsdp", None),
        P("section", "fsdp", None),
        P("section", "fsdp", None),
    )
    return jax.shard_map(body, mesh=mesh, in_specs=in_specs, out_specs=out_specs, check_vma=False)
```

```python
import functools
import math

import jax
import jax.numpy as jnp
from jax import lax
from jax.experimental import pallas as pl
from jax.experimental.pallas import tpu as pltpu
from jax.sharding import PartitionSpec as P

FRAMES = 16
LEVELS = 4
RING = 4
EPS = 1e-06
F32 = jnp.float32
BF16 = jnp.bfloat16
MESH = pl.DeviceIdType.MESH


def lookup_level(level_embed, level_index):
    onehot = (jnp.arange(LEVELS, dtype=jnp.int32) == level_index).astype(F32)
    return jnp.sum(onehot[:, None] * level_embed, axis=0)


def time_hidden(timesteps, level_row):
    half_width = level_row.shape[0] // 2
    frequency = jnp.exp(-math.log(10000.0) * jnp.arange(half_width, dtype=F32) / half_width)
    phases = timesteps.astype(F32)[:, None] * frequency[None, :]
    embedded = jnp.concatenate([jnp.sin(phases), jnp.cos(phases)], axis=-1) + level_row[None, :]
    return jax.nn.silu(embedded).astype(BF16)


def sigmoid(t):
    return 0.5 + 0.5 * jnp.tanh(0.5 * t)


def nt(a, b):
    return lax.dot_general(a, b, (((1,), (1,)), ((), ())), preferred_element_type=F32)


def dot(a, b):
    return jnp.dot(a, b, preferred_element_type=F32)


def tick(
    sections,
    hid, handoff, returning, stash, held, tw_in, pw_in, fw_in,
    out_f, out_b, out_skip, out_tg, out_pg, out_fg,
    arrived, back, stash_v, held_v, tw, pw, fwpad, hid_all, part, film_in, film,
    modf, modb, dtp, gated, gb, fout, bout, mod_t, gated_t, grad,
    ra_p, ra_m, rb_p, rb_m, zsend, zrecv, sums, dfilm, fg, tg, pg,
    load_sem, move_send, move_recv, hid_send, hid_recv, part_send, part_recv,
    df_send, df_recv, ag_send, ag_recv, skip_send, skip_recv, rs_send, rs_recv, out_sem, go,
):
    rows, ch = arrived.shape
    cell = rows // FRAMES
    chunk = rows // 4
    small = cell
    tws, pws, fws = tw_in.shape[1], pw_in.shape[1], fw_in.shape[1]
    n_fsdp = 2 * RING
    s, f = lax.axis_index("section"), lax.axis_index("fsdp")
    z, x = f // RING, f % RING
    xp, xm, x2 = (x + 1) % RING, (x + RING - 1) % RING, (x + 2) % RING
    zo = 1 - z
    fz, fxp, fxm = zo * RING + x, z * RING + xp, z * RING + xm
    ahead, behind, mirror = (s + 1) % sections, (s + sections - 1) % sections, sections - 1 - s
    core = s % 2
    sibling = s + 1 - 2 * core
    is_enc = s < sections // 2
    enc = jnp.where(is_enc, 1, 0)
    first = core == enc
    enc_f = enc.astype(F32)

    def at(section, fsdp):
        return {"section": section, "fsdp": fsdp}

    def remote(src, dst, send, recv, section, fsdp):
        return pltpu.make_async_remote_copy(
            src_ref=src, dst_ref=dst, send_sem=send, recv_sem=recv,
            device_id=at(section, fsdp), device_id_type=MESH,
        )

    fwpad[...] = jnp.zeros_like(fwpad)
    loads = [
        pltpu.make_async_copy(fw_in.at[0], fwpad.at[pl.ds(f * fws, fws)], load_sem.at[0]),
        pltpu.make_async_copy(stash.at[0], stash_v, load_sem.at[1]),
        pltpu.make_async_copy(held.at[0], held_v, load_sem.at[2]),
        pltpu.make_async_copy(tw_in.at[0], tw.at[pl.ds(f * tws, tws)], load_sem.at[3]),
        pltpu.make_async_copy(pw_in.at[0], pw.at[pl.ds(f * pws, pws)], load_sem.at[4]),
        pltpu.make_async_copy(hid, hid_all.at[:, f], load_sem.at[5]),
    ]
    for load in loads:
        load.start()

    barrier = pltpu.get_barrier_semaphore()
    for section in (ahead, behind, mirror):
        pl.semaphore_signal(barrier, inc=1, device_id=at(section, f), device_id_type=MESH)
    for d in range(1, n_fsdp):
        pl.semaphore_signal(barrier, inc=1, device_id=at(s, (f + d) % n_fsdp), device_id_type=MESH)
    pl.semaphore_wait(barrier, 3 + n_fsdp - 1)

    hid_out = [
        remote(hid, hid_all.at[:, f], hid_send.at[d], hid_recv.at[d], s, (f + d) % n_fsdp)
        for d in range(1, n_fsdp)
    ]
    for copy in hid_out:
        copy.start()

    h0 = {tws: (tws // 2 + 15) // 16 * 16, pws: pws // 2 // 16 * 16}

    def ag_copies(i, src_own, full, n):
        lo, hi = h0[n], n - h0[n]

        def shard(index):
            return full.at[pl.ds(index * n, n)]

        def low(index):
            return full.at[pl.ds(index * n, lo)]

        def high(index):
            return full.at[pl.ds(index * n + lo, hi)]

        fo_p, fo_m = zo * RING + xp, zo * RING + xm
        f_2, fo_2 = z * RING + x2, zo * RING + x2
        plan = [
            (src_own.at[0], shard(f), shard(fz), fz),
            (src_own.at[0], shard(f), shard(fxm), fxp),
            (src_own.at[0], shard(f), shard(fxp), fxm),
            (shard(fz), shard(fz), shard(fo_m), fxp),
            (shard(fz), shard(fz), shard(fo_p), fxm),
            (low(fxm), low(fxm), low(f_2), fxp),
            (high(fxp), high(fxp), high(f_2), fxm),
            (low(fo_m), low(fo_m), low(fo_2), fxp),
            (high(fo_p), high(fo_p), high(fo_2), fxm),
        ]
        sends, recvs = [], []
        for k, (src, dst, land, target) in enumerate(plan):
            sends.append(remote(src, dst, ag_send.at[i, k], ag_recv.at[i, k], s, target))
            recvs.append(remote(land, land, ag_send.at[i, k], ag_recv.at[i, k], s, target))
        return sends, recvs

    tw_sends, tw_recvs = ag_copies(0, tw_in, tw, tws)
    pw_sends, pw_recvs = ag_copies(1, pw_in, pw, pws)

    def ag_begin():
        for k in range(3):
            tw_sends[k].start()
        for k in range(3):
            pw_sends[k].start()

    pl.when(first)(ag_begin)

    move_f = remote(handoff.at[0], arrived, move_send.at[0], move_recv.at[0], ahead, f)
    move_b = remote(returning.at[0], back, move_send.at[1], move_recv.at[1], behind, f)
    move_f.start()
    move_b.start()

    for padded in (modf, modb, dtp):
        padded[0:cell] = jnp.zeros((cell, ch), BF16)
        padded[cell + rows : 2 * cell + rows] = jnp.zeros((cell, ch), BF16)

    loads[0].wait()
    loads[5].wait()
    for d in range(1, n_fsdp):
        came = (f + n_fsdp - d) % n_fsdp
        remote(hid, hid_all.at[:, came], hid_send.at[d], hid_recv.at[d], s, came).wait_recv()
    hidden = jnp.concatenate(
        [hid_all[r, j] for r in range(2) for j in range(n_fsdp)], axis=0
    ).astype(BF16)
    partial = dot(hidden, fwpad[...])
    for r in range(2):
        for j in range(n_fsdp):
            k = r * n_fsdp + j
            part[j, r] = partial[k : k + 1]
    part_out = []
    for d in range(1, n_fsdp):
        j = (f + d) % n_fsdp
        part_out.append(remote(part.at[j], film_in.at[f], part_send.at[d], part_recv.at[d], s, j))
    for copy in part_out:
        copy.start()
    for d in range(1, n_fsdp):
        came = (f + n_fsdp - d) % n_fsdp
        remote(part.at[came], film_in.at[came], part_send.at[d], part_recv.at[d], s, came).wait_recv()
    film_in[f] = part[f]
    film[...] = jnp.sum(film_in[...], axis=0)

    def scale_shift(r):
        return 1.0 + film[r, :, 0:ch], film[r, :, ch : 2 * ch]

    def modulate(read, r, dst):
        scale, shift = scale_shift(r)

        def step(i, carry):
            at_row = pl.multiple_of(i * small, small)
            v = read(at_row, small)
            rstd = lax.rsqrt(jnp.mean(v * v, axis=-1, keepdims=True) + EPS)
            dst[pl.ds(at_row + cell, small)] = (v * rstd * scale + shift).astype(BF16)
            return carry

        lax.fori_loop(0, rows // small, step, 0)

    def read_stash(r0, n):
        return stash_v[pl.ds(r0, n)].astype(F32)

    def read_forward(r0, n):
        return arrived[pl.ds(r0, n)].astype(F32) + held_v[pl.ds(r0, n)].astype(F32) * (1.0 - enc_f)

    def read_grad(r0, n):
        return back[pl.ds(r0, n)].astype(F32) + held_v[pl.ds(r0, n)].astype(F32) * enc_f

    loads[1].wait()
    loads[2].wait()
    modulate(read_stash, 1, modb)

    @pl.when(jnp.logical_not(first))
    def _():
        pl.semaphore_wait(go, 1)
        ag_begin()

    for recvs, sends in ((tw_recvs, tw_sends), (pw_recvs, pw_sends)):
        recvs[0].wait_recv()
        sends[3].start()
        sends[4].start()
    for recvs, sends in ((tw_recvs, tw_sends), (pw_recvs, pw_sends)):
        recvs[1].wait_recv()
        sends[5].start()
        recvs[2].wait_recv()
        sends[6].start()
    for recvs, sends in ((tw_recvs, tw_sends), (pw_recvs, pw_sends)):
        recvs[3].wait_recv()
        sends[7].start()
        recvs[4].wait_recv()
        sends[8].start()

    @pl.when(first)
    def _():
        pl.semaphore_signal(go, inc=1, device_id=at(sibling, f), device_id_type=MESH)

    loads[3].wait()
    loads[4].wait()

    def gather_end():
        for recvs in (tw_recvs, pw_recvs):
            for k in range(5, 9):
                recvs[k].wait_recv()

    def skip_copy(src, c):
        piece = pl.ds(pl.multiple_of(c * chunk, chunk), chunk)
        return remote(src.at[piece], out_skip.at[0, piece], skip_send.at[c], skip_recv.at[c], mirror, f)

    def temporal_of(mod, r0):
        taps = [mod[pl.ds(pl.multiple_of(r0 + k * cell, cell), chunk)] for k in range(3)]
        return dot(jnp.concatenate(taps, axis=1), tw[...])

    out_f_copy = pltpu.make_async_copy(fout, out_f.at[0], out_sem.at[0])
    out_b_copy = pltpu.make_async_copy(bout, out_b.at[0], out_sem.at[1])

    def forward():
        move_f.wait_recv()
        modulate(read_forward, 0, modf)
        pl.when(is_enc)(gather_end)

        def step(c, carry):
            r0 = pl.multiple_of(c * chunk, chunk)
            t = temporal_of(modf, r0)
            gate = (t * sigmoid(t)).astype(BF16)
            fout[pl.ds(r0, chunk)] = (read_forward(r0, chunk) + dot(gate, pw[...])).astype(BF16)

            @pl.when(is_enc)
            def _():
                skip_copy(fout, c).start()

            return carry

        lax.fori_loop(0, rows // chunk, step, 0)
        out_f_copy.start()

    half = (tws + pws) // 2
    lo, hi = pl.ds(0, half), pl.ds(half, half)
    rs_plan = [
        (grad.at[:, x2, lo], ra_p, fxp, fxm),
        (grad.at[:, x2, hi], ra_m, fxm, fxp),
        (grad.at[:, xp, hi], rb_p.at[:, hi], fxp, fxm),
        (grad.at[:, xm, lo], rb_m.at[:, lo], fxm, fxp),
        (ra_p, rb_p.at[:, lo], fxp, fxm),
        (ra_m, rb_m.at[:, hi], fxm, fxp),
        (zsend, zrecv, fz, fz),
    ]
    rs = [
        remote(src, dst, rs_send.at[k], rs_recv.at[k], s, target)
        for k, (src, dst, target, _) in enumerate(rs_plan)
    ]
    df_out = [
        remote(dfilm.at[f], dfilm.at[f], df_send.at[d], df_recv.at[d], s, (f + d) % n_fsdp)
        for d in range(1, n_fsdp)
    ]

    def backward():
        move_b.wait_recv()
        pl.when(jnp.logical_not(is_enc))(gather_end)
        sums[...] = jnp.zeros_like(sums)
        scale, _ = scale_shift(1)

        def step(c, carry):
            @pl.when(c < rows // chunk)
            def _():
                r0 = pl.multiple_of(c * chunk, chunk)
                t = temporal_of(modb, r0)
                sig = sigmoid(t)
                gated[pl.ds(r0, chunk)] = (t * sig).astype(BF16)
                g = read_grad(r0, chunk).astype(BF16)
                gb[pl.ds(r0, chunk)] = g
                dgate = nt(g, pw[...]).astype(BF16).astype(F32)
                dtp[pl.ds(pl.multiple_of(r0 + cell, cell), chunk)] = (
                    dgate * (sig * (1.0 + t * (1.0 - sig)))
                ).astype(BF16)

            @pl.when(c >= 1)
            def _():
                r0 = pl.multiple_of((c - 1) * chunk, chunk)
                dmod = jnp.zeros((chunk, ch), F32)
                for k in range(3):
                    piece = dtp[pl.ds(pl.multiple_of(r0 + (2 - k) * cell, cell), chunk)]
                    dmod += nt(piece, tw[k * ch : (k + 1) * ch])
                v = read_stash(r0, chunk)
                rstd = lax.rsqrt(jnp.mean(v * v, axis=-1, keepdims=True) + EPS)
                normalized = v * rstd
                sums[0] += jnp.sum((dmod * normalized).reshape(chunk // 8, 8, ch), axis=0)
                sums[1] += jnp.sum(dmod.reshape(chunk // 8, 8, ch), axis=0)
                dn = dmod * scale
                along = jnp.mean(dn * normalized, axis=-1, keepdims=True)
                bout[pl.ds(r0, chunk)] = (
                    read_grad(r0, chunk) + rstd * (dn - normalized * along)
                ).astype(BF16)

                @pl.when(jnp.logical_not(is_enc))
                def _():
                    skip_copy(bout, c - 1).start()

            return carry

        lax.fori_loop(0, rows // chunk + 1, step, 0)
        out_b_copy.start()
        dfilm[f] = jnp.concatenate(
            [jnp.sum(sums[0], axis=0, keepdims=True), jnp.sum(sums[1], axis=0, keepdims=True)], axis=1
        )
        for copy in df_out:
            copy.start()

        def turn(i, carry):
            cols = pl.ds(pl.multiple_of(i * 128, 128), 128)
            mod_t[cols] = modb[pl.ds(cell, rows), cols].T
            gated_t[cols] = gated[:, cols].T
            return carry

        lax.fori_loop(0, ch // 128, turn, 0)
        block = ch // 8
        for part_no in range(2):
            mrows = slice(part_no * ch // 2, (part_no + 1) * ch // 2)
            value = dot(gated_t[mrows], gb[...]).astype(BF16)
            for i in range(4):
                b = part_no * 4 + i
                grad[b // RING, b % RING, tws : tws + pws] = value[i * block : (i + 1) * block]
            for k in range(3):
                value = dot(mod_t[mrows], dtp[(2 - k) * cell : (2 - k) * cell + rows]).astype(BF16)
                for i in range(4):
                    b = k * 8 + part_no * 4 + i
                    j = b // 3
                    grad[j // RING, j % RING, (b % 3) * block : (b % 3 + 1) * block] = value[
                        i * block : (i + 1) * block
                    ]
        for k in range(4):
            rs[k].start()

    def phase(p, carry):
        which = p + enc
        pl.when(which == 1)(forward)
        pl.when(which != 1)(backward)
        return carry

    lax.fori_loop(0, 2, phase, 0)

    def add_rows(dst, src):
        for zi in range(2):
            dst[zi] = (dst[zi].astype(F32) + src[zi].astype(F32)).astype(BF16)

    rs[0].wait_recv()
    add_rows(ra_p, grad.at[:, xp, lo])
    rs[4].start()
    rs[1].wait_recv()
    add_rows(ra_m, grad.at[:, xm, hi])
    rs[5].start()

    for d in range(1, n_fsdp):
        came = (f + n_fsdp - d) % n_fsdp
        remote(dfilm.at[came], dfilm.at[came], df_send.at[d], df_recv.at[d], s, came).wait_recv()
    hidden_b = jnp.concatenate([hid_all[1, j] for j in range(n_fsdp)], axis=0).astype(BF16)
    dfilm_all = jnp.concatenate([dfilm[j] for j in range(n_fsdp)], axis=0).astype(BF16)
    fg[...] = lax.dot_general(hidden_b, dfilm_all, (((0,), (0,)), ((), ())), preferred_element_type=F32)
    fg_copy = pltpu.make_async_copy(fg.at[pl.ds(f * fws, fws)], out_fg.at[0], out_sem.at[2])
    fg_copy.start()

    for k in range(2, 6):
        rs[k].wait_recv()

    def along_x(zi):
        return grad[zi, x].astype(F32) + rb_p[zi].astype(F32) + rb_m[zi].astype(F32)

    zsend[...] = along_x(zo).astype(BF16)
    rs[6].start()
    own = along_x(z)
    tg[...] = own[0:tws]
    pg[...] = own[tws : tws + pws]
    rs[6].wait_recv()
    tg[...] += zrecv[0:tws].astype(F32)
    pg[...] += zrecv[tws : tws + pws].astype(F32)
    tg_copy = pltpu.make_async_copy(tg, out_tg.at[0], out_sem.at[3])
    pg_copy = pltpu.make_async_copy(pg, out_pg.at[0], out_sem.at[4])
    tg_copy.start()
    pg_copy.start()

    for copy in hid_out + part_out + df_out + tw_sends + pw_sends + rs + [move_f, move_b]:
        copy.wait_send()

    def skip_end(c, carry):
        copy = skip_copy(fout, c)
        copy.wait_send()
        copy.wait_recv()
        return carry

    lax.fori_loop(0, rows // chunk, skip_end, 0)
    for copy in (out_f_copy, out_b_copy, fg_copy, tg_copy, pg_copy):
        copy.wait()


def body(
    handoff,
    returning,
    stashed_input,
    skip_held,
    timesteps_forward,
    timesteps_backward,
    section_level,
    level_embed,
    temporal_weight,
    point_weight,
    film_weight,
):
    sections, n_fsdp = lax.axis_size("section"), lax.axis_size("fsdp")
    _, rows, ch = handoff.shape
    tws, pws, fws = temporal_weight.shape[1], point_weight.shape[1], film_weight.shape[1]
    embed = level_embed.shape[1]
    cell = rows // FRAMES
    level_row = lookup_level(level_embed, section_level[0])
    steps = jnp.concatenate([timesteps_forward[0], timesteps_backward[0]])
    hid = time_hidden(steps, level_row).astype(F32)[:, None, :]

    def vmem(shape, dtype=BF16):
        return pltpu.VMEM(shape, dtype)

    act, padded = (rows, ch), (rows + 2 * cell, ch)
    shard, half = (tws + pws, ch), ((tws + pws) // 2, ch)
    dma = pltpu.SemaphoreType.DMA
    scratch = [
        vmem(act), vmem(act), vmem(act), vmem(act),
        vmem((tws * n_fsdp, ch)), vmem((pws * n_fsdp, ch)), vmem((embed, 2 * ch)),
        vmem((2, n_fsdp, 1, embed), F32),
        vmem((n_fsdp, 2, 1, 2 * ch), F32), vmem((n_fsdp, 2, 1, 2 * ch), F32), vmem((2, 1, 2 * ch), F32),
        vmem(padded), vmem(padded), vmem(padded),
        vmem(act), vmem(act), vmem(act), vmem(act),
        vmem((ch, rows)), vmem((ch, rows)),
        vmem((2, RING) + shard),
        vmem((2,) + half), vmem((2,) + half), vmem((2,) + shard), vmem((2,) + shard),
        vmem(shard), vmem(shard),
        vmem((2, 8, ch), F32), vmem((n_fsdp, 1, 2 * ch), F32),
        vmem((embed, 2 * ch), F32), vmem((tws, ch), F32), vmem((pws, ch), F32),
        dma((6,)), dma((2,)), dma((2,)), dma((n_fsdp,)), dma((n_fsdp,)), dma((n_fsdp,)), dma((n_fsdp,)),
        dma((n_fsdp,)), dma((n_fsdp,)), dma((2, 9)), dma((2, 9)), dma((4,)), dma((4,)), dma((7,)), dma((7,)),
        dma((5,)), pltpu.SemaphoreType.REGULAR,
    ]
    hbm = pl.BlockSpec(memory_space=pl.ANY)
    local = pl.BlockSpec(memory_space=pltpu.VMEM)
    like = jax.ShapeDtypeStruct
    return tuple(
        pl.pallas_call(
            functools.partial(tick, sections),
            out_shape=(
                like(handoff.shape, BF16),
                like(handoff.shape, BF16),
                like(handoff.shape, BF16),
                like(temporal_weight.shape, F32),
                like(point_weight.shape, F32),
                like(film_weight.shape, F32),
            ),
            in_specs=[local] + [hbm] * 7,
            out_specs=(hbm,) * 6,
            scratch_shapes=scratch,
            compiler_params=pltpu.CompilerParams(
                collective_id=0, has_side_effects=True, vmem_limit_bytes=56 * 1024 * 1024
            ),
            name="relay_tick",
        )(hid, handoff, returning, stashed_input, skip_held, temporal_weight, point_weight, film_weight)
    )


def solution(mesh):
    rows = P("section", "fsdp", None)
    in_specs = (rows, rows, rows, rows, P("section", "fsdp"), P("section", "fsdp"), P("section"), P(), rows, rows, rows)
    return jax.shard_map(body, mesh=mesh, in_specs=in_specs, out_specs=(rows,) * 6, check_vma=False)
```

```python
import functools
import math

import jax
import jax.numpy as jnp
from jax import lax
from jax.experimental import pallas as pl
from jax.experimental.pallas import tpu as pltpu
from jax.sharding import PartitionSpec as P

FRAMES = 16
LEVELS = 4
RING = 4
EPS = 1e-06
F32 = jnp.float32
BF16 = jnp.bfloat16
MESH = pl.DeviceIdType.MESH


def lookup_level(level_embed, level_index):
    onehot = (jnp.arange(LEVELS, dtype=jnp.int32) == level_index).astype(F32)
    return jnp.sum(onehot[:, None] * level_embed, axis=0)


def time_hidden(timesteps, level_row):
    half_width = level_row.shape[0] // 2
    frequency = jnp.exp(-math.log(10000.0) * jnp.arange(half_width, dtype=F32) / half_width)
    phases = timesteps.astype(F32)[:, None] * frequency[None, :]
    embedded = jnp.concatenate([jnp.sin(phases), jnp.cos(phases)], axis=-1) + level_row[None, :]
    return jax.nn.silu(embedded).astype(BF16)


def sigmoid(t):
    return 0.5 + 0.5 * jnp.tanh(0.5 * t)


def nt(a, b):
    return lax.dot_general(a, b, (((1,), (1,)), ((), ())), preferred_element_type=F32)


def dot(a, b):
    return jnp.dot(a, b, preferred_element_type=F32)


def tick(
    sections,
    hid, handoff, returning, stash, held, tw_in, pw_in, fw_in,
    out_f, out_b, out_skip, out_tg, out_pg, out_fg,
    arrived, back, stash_v, held_v, tw, pw, fwpad, hid_all, part, film_in, film,
    modf, modb, dtp, gated, gb, fout, bout, mod_t, gated_t, grad,
    ra_p, ra_m, rb_p, rb_m, zsend, zrecv, sums, dfilm, fg, tg, pg, relay_h, relay_r,
    load_sem, move_send, move_recv, hid_send, hid_recv, part_send, part_recv,
    df_send, df_recv, ag_send, ag_recv, skip_send, skip_recv, rs_send, rs_recv, out_sem,
    relay_send, relay_recv, go,
):
    rows, ch = arrived.shape
    cell = rows // FRAMES
    chunk = rows // 4
    small = cell
    tws, pws, fws = tw_in.shape[1], pw_in.shape[1], fw_in.shape[1]
    n_fsdp = 2 * RING
    s, f = lax.axis_index("section"), lax.axis_index("fsdp")
    z, x = f // RING, f % RING
    xp, xm, x2 = (x + 1) % RING, (x + RING - 1) % RING, (x + 2) % RING
    zo = 1 - z
    fz, fxp, fxm = zo * RING + x, z * RING + xp, z * RING + xm
    ahead, behind, mirror = (s + 1) % sections, (s + sections - 1) % sections, sections - 1 - s
    core = s % 2
    sibling = s + 1 - 2 * core
    is_enc = s < sections // 2
    enc = jnp.where(is_enc, 1, 0)
    first = core == enc
    enc_f = enc.astype(F32)
    forward_first = enc * jnp.where(first, 1, 0)

    period = min(8, sections)
    place, run = s % period, s // period
    enc_before = jnp.where((s + sections - 1) % sections < sections // 2, 1, 0)
    enc_after = jnp.where((s + 1) % sections < sections // 2, 1, 0)
    far_f, far_b = place == period - 1, place == 0
    near_f, near_b = jnp.logical_not(far_f), jnp.logical_not(far_b)
    relay_f_at, relay_b_at = run * period + enc, run * period + period - 2 + enc
    is_relay_f, is_relay_b = s == relay_f_at, s == relay_b_at
    relay_f_from, relay_b_from = run * period + period - 1, run * period
    relay_f_to, relay_b_to = (run * period + period) % sections, (run * period + sections - 1) % sections
    relay_f_into = (run * period + sections - period) % sections + enc_before
    relay_b_into = (run * period + period) % sections + period - 2 + enc_after

    def at(section, fsdp):
        return {"section": section, "fsdp": fsdp}

    def remote(src, dst, send, recv, section, fsdp):
        return pltpu.make_async_remote_copy(
            src_ref=src, dst_ref=dst, send_sem=send, recv_sem=recv,
            device_id=at(section, fsdp), device_id_type=MESH,
        )

    fwpad[...] = jnp.zeros_like(fwpad)
    loads = [
        pltpu.make_async_copy(fw_in.at[0], fwpad.at[pl.ds(f * fws, fws)], load_sem.at[0]),
        pltpu.make_async_copy(stash.at[0], stash_v, load_sem.at[1]),
        pltpu.make_async_copy(held.at[0], held_v, load_sem.at[2]),
        pltpu.make_async_copy(tw_in.at[0], tw.at[pl.ds(f * tws, tws)], load_sem.at[3]),
        pltpu.make_async_copy(pw_in.at[0], pw.at[pl.ds(f * pws, pws)], load_sem.at[4]),
        pltpu.make_async_copy(hid, hid_all.at[:, f], load_sem.at[5]),
    ]
    for load in loads:
        load.start()

    barrier = pltpu.get_barrier_semaphore()
    for section in (ahead, behind, mirror):
        pl.semaphore_signal(barrier, inc=1, device_id=at(section, f), device_id_type=MESH)
    for d in range(1, n_fsdp):
        pl.semaphore_signal(barrier, inc=1, device_id=at(s, (f + d) % n_fsdp), device_id_type=MESH)
    greet = [(is_relay_f, relay_f_from), (is_relay_b, relay_b_from), (far_b, relay_f_into), (far_f, relay_b_into)]
    for role, section in greet:
        pl.when(role)(
            functools.partial(
                pl.semaphore_signal, barrier, inc=1, device_id=at(section, f), device_id_type=MESH
            )
        )
    extra = sum(jnp.where(role, 1, 0) for role in (far_f, far_b, is_relay_f, is_relay_b))
    pl.semaphore_wait(barrier, 3 + n_fsdp - 1 + extra)

    hid_out = [
        remote(hid, hid_all.at[:, f], hid_send.at[d], hid_recv.at[d], s, (f + d) % n_fsdp)
        for d in range(1, n_fsdp)
    ]
    for copy in hid_out:
        copy.start()

    h0 = {tws: (tws // 2 + 15) // 16 * 16, pws: pws // 2 // 16 * 16}

    def ag_copies(i, src_own, full, n):
        lo, hi = h0[n], n - h0[n]

        def shard(index):
            return full.at[pl.ds(index * n, n)]

        def low(index):
            return full.at[pl.ds(index * n, lo)]

        def high(index):
            return full.at[pl.ds(index * n + lo, hi)]

        fo_p, fo_m = zo * RING + xp, zo * RING + xm
        f_2, fo_2 = z * RING + x2, zo * RING + x2
        plan = [
            (src_own.at[0], shard(f), shard(fz), fz),
            (src_own.at[0], shard(f), shard(fxm), fxp),
            (src_own.at[0], shard(f), shard(fxp), fxm),
            (shard(fz), shard(fz), shard(fo_m), fxp),
            (shard(fz), shard(fz), shard(fo_p), fxm),
            (low(fxm), low(fxm), low(f_2), fxp),
            (high(fxp), high(fxp), high(f_2), fxm),
            (low(fo_m), low(fo_m), low(fo_2), fxp),
            (high(fo_p), high(fo_p), high(fo_2), fxm),
        ]
        sends, recvs = [], []
        for k, (src, dst, land, target) in enumerate(plan):
            sends.append(remote(src, dst, ag_send.at[i, k], ag_recv.at[i, k], s, target))
            recvs.append(remote(land, land, ag_send.at[i, k], ag_recv.at[i, k], s, target))
        return sends, recvs

    tw_sends, tw_recvs = ag_copies(0, tw_in, tw, tws)
    pw_sends, pw_recvs = ag_copies(1, pw_in, pw, pws)

    def start(pairs, ks):
        for k in ks:
            for sends in pairs:
                sends[k].start()

    both = (tw_sends, pw_sends)
    later = jnp.logical_not(first)

    @pl.when(first)
    def _():
        start(both, (0,))
        start((tw_sends,), (1, 2))
        start((pw_sends,), (1, 2))

    upper, lower = pl.ds(0, rows // 2), pl.ds(rows // 2, rows // 2)
    move_fa = remote(handoff.at[0, upper], arrived.at[upper], move_send.at[0], move_recv.at[0], ahead, f)
    move_fb = remote(handoff.at[0, lower], arrived.at[lower], move_send.at[1], move_recv.at[1], ahead, f)
    move_fr = remote(handoff.at[0, lower], relay_h, move_send.at[1], relay_recv.at[0], relay_f_at, f)
    pass_f = remote(relay_h, arrived.at[lower], relay_send.at[0], move_recv.at[1], relay_f_to, f)
    move_ba = remote(returning.at[0, upper], back.at[upper], move_send.at[2], move_recv.at[2], behind, f)
    move_bb = remote(returning.at[0, lower], back.at[lower], move_send.at[3], move_recv.at[3], behind, f)
    move_br = remote(returning.at[0, lower], relay_r, move_send.at[3], relay_recv.at[1], relay_b_at, f)
    pass_b = remote(relay_r, back.at[lower], relay_send.at[1], move_recv.at[3], relay_b_to, f)

    @pl.when(near_f)
    def _():
        move_fa.start()
        move_fb.start()

    @pl.when(near_b)
    def _():
        move_ba.start()
        move_bb.start()

    pl.when(far_f)(move_fr.start)
    pl.when(far_b)(move_br.start)

    for padded in (modf, modb, dtp):
        padded[0:cell] = jnp.zeros((cell, ch), BF16)
        padded[cell + rows : 2 * cell + rows] = jnp.zeros((cell, ch), BF16)

    loads[0].wait()
    loads[5].wait()
    for d in range(1, n_fsdp):
        came = (f + n_fsdp - d) % n_fsdp
        remote(hid, hid_all.at[:, came], hid_send.at[d], hid_recv.at[d], s, came).wait_recv()
    hidden = jnp.concatenate(
        [hid_all[r, j] for r in range(2) for j in range(n_fsdp)], axis=0
    ).astype(BF16)
    partial = dot(hidden, fwpad[...])
    for r in range(2):
        for j in range(n_fsdp):
            k = r * n_fsdp + j
            part[j, r] = partial[k : k + 1]
    part_out = []
    for d in range(1, n_fsdp):
        j = (f + d) % n_fsdp
        part_out.append(remote(part.at[j], film_in.at[f], part_send.at[d], part_recv.at[d], s, j))
    for copy in part_out:
        copy.start()

    @pl.when(later)
    def _():
        start(both, (0,))

    for recvs, sends in ((tw_recvs, tw_sends), (pw_recvs, pw_sends)):
        recvs[0].wait_recv()
        pl.when(first)(functools.partial(start, (sends,), (3, 4)))
    pl.when(far_f)(move_fa.start)
    pl.when(far_b)(move_ba.start)
    for d in range(1, n_fsdp):
        came = (f + n_fsdp - d) % n_fsdp
        remote(part.at[came], film_in.at[came], part_send.at[d], part_recv.at[d], s, came).wait_recv()
    film_in[f] = part[f]
    film[...] = jnp.sum(film_in[...], axis=0)

    def scale_shift(r):
        return 1.0 + film[r, :, 0:ch], film[r, :, ch : 2 * ch]

    def modulate(read, r, dst):
        scale, shift = scale_shift(r)

        def step(i, carry):
            at_row = pl.multiple_of(i * small, small)
            v = read(at_row, small)
            rstd = lax.rsqrt(jnp.mean(v * v, axis=-1, keepdims=True) + EPS)
            dst[pl.ds(at_row + cell, small)] = (v * rstd * scale + shift).astype(BF16)
            return carry

        lax.fori_loop(0, rows // small, step, 0)

    def read_stash(r0, n):
        return stash_v[pl.ds(r0, n)].astype(F32)

    def read_forward(r0, n):
        return arrived[pl.ds(r0, n)].astype(F32) + held_v[pl.ds(r0, n)].astype(F32) * (1.0 - enc_f)

    def read_grad(r0, n):
        return back[pl.ds(r0, n)].astype(F32) + held_v[pl.ds(r0, n)].astype(F32) * enc_f

    loads[1].wait()
    loads[2].wait()
    modulate(read_stash, 1, modb)

    @pl.when(later)
    def _():
        pl.semaphore_wait(go, 1)
        for sends in both:
            start((sends,), (1, 2, 3, 4))

    for recvs, sends in ((tw_recvs, tw_sends), (pw_recvs, pw_sends)):
        recvs[1].wait_recv()
        sends[5].start()
        recvs[2].wait_recv()
        sends[6].start()
    for recvs, sends in ((tw_recvs, tw_sends), (pw_recvs, pw_sends)):
        recvs[3].wait_recv()
        sends[7].start()
        recvs[4].wait_recv()
        sends[8].start()

    @pl.when(first)
    def _():
        pl.semaphore_signal(go, inc=1, device_id=at(sibling, f), device_id_type=MESH)

    @pl.when(is_relay_f)
    def _():
        move_fr.wait_recv()
        pass_f.start()

    @pl.when(is_relay_b)
    def _():
        move_br.wait_recv()
        pass_b.start()

    loads[3].wait()
    loads[4].wait()

    def gather_end():
        for recvs in (tw_recvs, pw_recvs):
            for k in range(5, 9):
                recvs[k].wait_recv()

    def skip_copy(src, c):
        piece = pl.ds(pl.multiple_of(c * chunk, chunk), chunk)
        return remote(src.at[piece], out_skip.at[0, piece], skip_send.at[c], skip_recv.at[c], mirror, f)

    def temporal_of(mod, r0):
        taps = [mod[pl.ds(pl.multiple_of(r0 + k * cell, cell), chunk)] for k in range(3)]
        return dot(jnp.concatenate(taps, axis=1), tw[...])

    out_f_copy = pltpu.make_async_copy(fout, out_f.at[0], out_sem.at[0])
    out_b_copy = pltpu.make_async_copy(bout, out_b.at[0], out_sem.at[1])

    def forward():
        move_fa.wait_recv()
        move_fb.wait_recv()
        modulate(read_forward, 0, modf)
        pl.when(forward_first == 1)(gather_end)

        def step(c, carry):
            r0 = pl.multiple_of(c * chunk, chunk)
            t = temporal_of(modf, r0)
            gate = (t * sigmoid(t)).astype(BF16)
            fout[pl.ds(r0, chunk)] = (read_forward(r0, chunk) + dot(gate, pw[...])).astype(BF16)

            @pl.when(is_enc)
            def _():
                skip_copy(fout, c).start()

            return carry

        lax.fori_loop(0, rows // chunk, step, 0)
        out_f_copy.start()

    half = (tws + pws) // 2
    lo, hi = pl.ds(0, half), pl.ds(half, half)
    rs_plan = []
    for zi in (zo, z):
        rs_plan += [
            (grad.at[zi, x2, lo], ra_p.at[zi], fxp, fxm),
            (grad.at[zi, x2, hi], ra_m.at[zi], fxm, fxp),
            (grad.at[zi, xp, hi], rb_p.at[zi, hi], fxp, fxm),
            (grad.at[zi, xm, lo], rb_m.at[zi, lo], fxm, fxp),
            (ra_p.at[zi], rb_p.at[zi, lo], fxp, fxm),
            (ra_m.at[zi], rb_m.at[zi, hi], fxm, fxp),
        ]
    rs_plan.append((zsend, zrecv, fz, fz))
    rs = [
        remote(src, dst, rs_send.at[k], rs_recv.at[k], s, target)
        for k, (src, dst, target, _) in enumerate(rs_plan)
    ]
    df_out = [
        remote(dfilm.at[f], dfilm.at[f], df_send.at[d], df_recv.at[d], s, (f + d) % n_fsdp)
        for d in range(1, n_fsdp)
    ]

    def backward():
        move_ba.wait_recv()
        move_bb.wait_recv()
        pl.when(forward_first == 0)(gather_end)
        sums[...] = jnp.zeros_like(sums)
        scale, _ = scale_shift(1)

        def step(c, carry):
            @pl.when(c < rows // chunk)
            def _():
                r0 = pl.multiple_of(c * chunk, chunk)
                t = temporal_of(modb, r0)
                sig = sigmoid(t)
                gated[pl.ds(r0, chunk)] = (t * sig).astype(BF16)
                g = read_grad(r0, chunk).astype(BF16)
                gb[pl.ds(r0, chunk)] = g
                dgate = nt(g, pw[...]).astype(BF16).astype(F32)
                dtp[pl.ds(pl.multiple_of(r0 + cell, cell), chunk)] = (
                    dgate * (sig * (1.0 + t * (1.0 - sig)))
                ).astype(BF16)

            @pl.when(c >= 1)
            def _():
                r0 = pl.multiple_of((c - 1) * chunk, chunk)
                dmod = jnp.zeros((chunk, ch), F32)
                for k in range(3):
                    piece = dtp[pl.ds(pl.multiple_of(r0 + (2 - k) * cell, cell), chunk)]
                    dmod += nt(piece, tw[k * ch : (k + 1) * ch])
                v = read_stash(r0, chunk)
                rstd = lax.rsqrt(jnp.mean(v * v, axis=-1, keepdims=True) + EPS)
                normalized = v * rstd
                sums[0] += jnp.sum((dmod * normalized).reshape(chunk // 8, 8, ch), axis=0)
                sums[1] += jnp.sum(dmod.reshape(chunk // 8, 8, ch), axis=0)
                dn = dmod * scale
                along = jnp.mean(dn * normalized, axis=-1, keepdims=True)
                bout[pl.ds(r0, chunk)] = (
                    read_grad(r0, chunk) + rstd * (dn - normalized * along)
                ).astype(BF16)

                @pl.when(jnp.logical_not(is_enc))
                def _():
                    skip_copy(bout, c - 1).start()

            return carry

        lax.fori_loop(0, rows // chunk + 1, step, 0)
        out_b_copy.start()
        dfilm[f] = jnp.concatenate(
            [jnp.sum(sums[0], axis=0, keepdims=True), jnp.sum(sums[1], axis=0, keepdims=True)], axis=1
        )
        for copy in df_out:
            copy.start()

        def turn(i, carry):
            cols = pl.ds(pl.multiple_of(i * 128, 128), 128)
            mod_t[cols] = modb[pl.ds(cell, rows), cols].T
            gated_t[cols] = gated[:, cols].T
            return carry

        lax.fori_loop(0, ch // 128, turn, 0)
        block = ch // 8
        for part_no in range(2):
            mrows = slice(part_no * ch // 2, (part_no + 1) * ch // 2)
            value = dot(gated_t[mrows], gb[...]).astype(BF16)
            for i in range(4):
                b = part_no * 4 + i
                grad[b // RING, b % RING, tws : tws + pws] = value[i * block : (i + 1) * block]
            for k in range(3):
                value = dot(mod_t[mrows], dtp[(2 - k) * cell : (2 - k) * cell + rows]).astype(BF16)
                for i in range(4):
                    b = k * 8 + part_no * 4 + i
                    j = b // 3
                    grad[j // RING, j % RING, (b % 3) * block : (b % 3 + 1) * block] = value[
                        i * block : (i + 1) * block
                    ]
        for k in (0, 1, 2, 3, 6, 7, 8, 9):
            rs[k].start()

    def phase(p, carry):
        which = p + forward_first
        pl.when(which == 1)(forward)
        pl.when(which != 1)(backward)
        return carry

    lax.fori_loop(0, 2, phase, 0)

    def add_on(dst, src):
        dst[...] = (dst[...].astype(F32) + src[...].astype(F32)).astype(BF16)

    for k, zi in ((0, zo), (6, z)):
        rs[k].wait_recv()
        add_on(ra_p.at[zi], grad.at[zi, xp, lo])
        rs[k + 4].start()
        rs[k + 1].wait_recv()
        add_on(ra_m.at[zi], grad.at[zi, xm, hi])
        rs[k + 5].start()

    for d in range(1, n_fsdp):
        came = (f + n_fsdp - d) % n_fsdp
        remote(dfilm.at[came], dfilm.at[came], df_send.at[d], df_recv.at[d], s, came).wait_recv()
    hidden_b = jnp.concatenate([hid_all[1, j] for j in range(n_fsdp)], axis=0).astype(BF16)
    dfilm_all = jnp.concatenate([dfilm[j] for j in range(n_fsdp)], axis=0).astype(BF16)
    fg[...] = lax.dot_general(hidden_b, dfilm_all, (((0,), (0,)), ((), ())), preferred_element_type=F32)
    fg_copy = pltpu.make_async_copy(fg.at[pl.ds(f * fws, fws)], out_fg.at[0], out_sem.at[2])
    fg_copy.start()

    def along_x(zi):
        return grad[zi, x].astype(F32) + rb_p[zi].astype(F32) + rb_m[zi].astype(F32)

    for k in range(2, 6):
        rs[k].wait_recv()
    zsend[...] = along_x(zo).astype(BF16)
    rs[12].start()
    for k in range(8, 12):
        rs[k].wait_recv()
    own = along_x(z)
    tg[...] = own[0:tws]
    pg[...] = own[tws : tws + pws]
    rs[12].wait_recv()
    tg[...] += zrecv[0:tws].astype(F32)
    pg[...] += zrecv[tws : tws + pws].astype(F32)
    tg_copy = pltpu.make_async_copy(tg, out_tg.at[0], out_sem.at[3])
    pg_copy = pltpu.make_async_copy(pg, out_pg.at[0], out_sem.at[4])
    tg_copy.start()
    pg_copy.start()

    for copy in hid_out + part_out + df_out + tw_sends + pw_sends + rs + [move_fa, move_fb, move_ba, move_bb]:
        copy.wait_send()
    pl.when(is_relay_f)(pass_f.wait_send)
    pl.when(is_relay_b)(pass_b.wait_send)

    def skip_end(c, carry):
        copy = skip_copy(fout, c)
        copy.wait_send()
        copy.wait_recv()
        return carry

    lax.fori_loop(0, rows // chunk, skip_end, 0)
    for copy in (out_f_copy, out_b_copy, fg_copy, tg_copy, pg_copy):
        copy.wait()


def settle(*refs):
    sources, results, held, sem_in, sem_out = refs[:6], refs[6:12], refs[12:18], refs[18], refs[19]
    pieces = []
    for k in range(6):
        count = 4 if k < 3 else 1
        n = sources[k].shape[1] // count
        pieces += [(k, pl.ds(i * n, n)) for i in range(count)]
    loads = [
        pltpu.make_async_copy(sources[k].at[:, piece], held[k].at[:, piece], sem_in.at[i])
        for i, (k, piece) in enumerate(pieces)
    ]
    stores = [
        pltpu.make_async_copy(held[k].at[:, piece], results[k].at[:, piece], sem_out.at[i])
        for i, (k, piece) in enumerate(pieces)
    ]
    for load in loads:
        load.start()
    for load, store in zip(loads, stores):
        load.wait()
        store.start()
    for store in stores:
        store.wait()


def body(
    handoff,
    returning,
    stashed_input,
    skip_held,
    timesteps_forward,
    timesteps_backward,
    section_level,
    level_embed,
    temporal_weight,
    point_weight,
    film_weight,
):
    sections, n_fsdp = lax.axis_size("section"), lax.axis_size("fsdp")
    _, rows, ch = handoff.shape
    tws, pws, fws = temporal_weight.shape[1], point_weight.shape[1], film_weight.shape[1]
    embed = level_embed.shape[1]
    cell = rows // FRAMES
    level_row = lookup_level(level_embed, section_level[0])
    steps = jnp.concatenate([timesteps_forward[0], timesteps_backward[0]])
    hid = time_hidden(steps, level_row).astype(F32)[:, None, :]

    def vmem(shape, dtype=BF16):
        return pltpu.VMEM(shape, dtype)

    act, padded = (rows, ch), (rows + 2 * cell, ch)
    shard, half = (tws + pws, ch), ((tws + pws) // 2, ch)
    dma = pltpu.SemaphoreType.DMA
    scratch = [
        vmem(act), vmem(act), vmem(act), vmem(act),
        vmem((tws * n_fsdp, ch)), vmem((pws * n_fsdp, ch)), vmem((embed, 2 * ch)),
        vmem((2, n_fsdp, 1, embed), F32),
        vmem((n_fsdp, 2, 1, 2 * ch), F32), vmem((n_fsdp, 2, 1, 2 * ch), F32), vmem((2, 1, 2 * ch), F32),
        vmem(padded), vmem(padded), vmem(padded),
        vmem(act), vmem(act), vmem(act), vmem(act),
        vmem((ch, rows)), vmem((ch, rows)),
        vmem((2, RING) + shard),
        vmem((2,) + half), vmem((2,) + half), vmem((2,) + shard), vmem((2,) + shard),
        vmem(shard), vmem(shard),
        vmem((2, 8, ch), F32), vmem((n_fsdp, 1, 2 * ch), F32),
        vmem((embed, 2 * ch), F32), vmem((tws, ch), F32), vmem((pws, ch), F32),
        vmem((rows // 2, ch)), vmem((rows // 2, ch)),
        dma((6,)), dma((4,)), dma((4,)), dma((n_fsdp,)), dma((n_fsdp,)), dma((n_fsdp,)), dma((n_fsdp,)),
        dma((n_fsdp,)), dma((n_fsdp,)), dma((2, 9)), dma((2, 9)), dma((4,)), dma((4,)), dma((13,)), dma((13,)),
        dma((5,)), dma((2,)), dma((2,)), pltpu.SemaphoreType.REGULAR,
    ]
    hbm = pl.BlockSpec(memory_space=pl.ANY)
    local = pl.BlockSpec(memory_space=pltpu.VMEM)
    like = jax.ShapeDtypeStruct
    shapes = (
        like(handoff.shape, BF16),
        like(handoff.shape, BF16),
        like(handoff.shape, BF16),
        like(temporal_weight.shape, F32),
        like(point_weight.shape, F32),
        like(film_weight.shape, F32),
    )
    made = pl.pallas_call(
        functools.partial(tick, sections),
        out_shape=shapes,
        in_specs=[local] + [hbm] * 7,
        out_specs=(hbm,) * 6,
        scratch_shapes=scratch,
        compiler_params=pltpu.CompilerParams(
            collective_id=0, has_side_effects=True, vmem_limit_bytes=56 * 1024 * 1024
        ),
        name="relay_tick",
    )(hid, handoff, returning, stashed_input, skip_held, temporal_weight, point_weight, film_weight)
    return tuple(
        pl.pallas_call(
            settle,
            out_shape=shapes,
            in_specs=[hbm] * 6,
            out_specs=(hbm,) * 6,
            scratch_shapes=[vmem(out.shape, out.dtype) for out in shapes] + [dma((15,)), dma((15,))],
            compiler_params=pltpu.CompilerParams(vmem_limit_bytes=60 * 1024 * 1024),
            name="settle",
        )(*made)
    )


def solution(mesh):
    rows = P("section", "fsdp", None)
    in_specs = (rows, rows, rows, rows, P("section", "fsdp"), P("section", "fsdp"), P("section"), P(), rows, rows, rows)
    return jax.shard_map(body, mesh=mesh, in_specs=in_specs, out_specs=(rows,) * 6, check_vma=False)
```

```python
import functools
import math

import jax
import jax.numpy as jnp
from jax import lax
from jax.experimental import pallas as pl
from jax.experimental.pallas import tpu as pltpu
from jax.sharding import PartitionSpec as P

FRAMES = 16
LEVELS = 4
RING = 4
EPS = 1e-06
F32 = jnp.float32
BF16 = jnp.bfloat16
MESH = pl.DeviceIdType.MESH


def lookup_level(level_embed, level_index):
    onehot = (jnp.arange(LEVELS, dtype=jnp.int32) == level_index).astype(F32)
    return jnp.sum(onehot[:, None] * level_embed, axis=0)


def time_hidden(timesteps, level_row):
    half_width = level_row.shape[0] // 2
    frequency = jnp.exp(-math.log(10000.0) * jnp.arange(half_width, dtype=F32) / half_width)
    phases = timesteps.astype(F32)[:, None] * frequency[None, :]
    embedded = jnp.concatenate([jnp.sin(phases), jnp.cos(phases)], axis=-1) + level_row[None, :]
    return jax.nn.silu(embedded).astype(BF16)


def sigmoid(t):
    return 0.5 + 0.5 * jnp.tanh(0.5 * t)


def nt(a, b):
    return lax.dot_general(a, b, (((1,), (1,)), ((), ())), preferred_element_type=F32)


def dot(a, b):
    return jnp.dot(a, b, preferred_element_type=F32)


def tick(
    sections,
    hid, handoff, returning, stash, held, tw_in, pw_in, fw_in,
    out_f, out_b, out_skip, out_tg, out_pg, out_fg,
    arrived, back, stash_v, held_v, tw, pw, fwpad, hid_all, part, film_in, film,
    modf, modb, dtp, gated, gb, fout, bout, mod_t, gated_t, grad,
    ra_p, ra_m, rb_p, rb_m, zsend, zrecv, sums, dfilm, fg, tg, pg, relay_h, relay_r,
    load_sem, move_send, move_recv, hid_send, hid_recv, part_send, part_recv,
    df_send, df_recv, ag_send, ag_recv, skip_send, skip_recv, rs_send, rs_recv, out_sem,
    relay_send, relay_recv, go,
):
    rows, ch = arrived.shape
    cell = rows // FRAMES
    chunk = rows // 8
    small = cell
    tws, pws, fws = tw_in.shape[1], pw_in.shape[1], fw_in.shape[1]
    n_fsdp = 2 * RING
    s, f = lax.axis_index("section"), lax.axis_index("fsdp")
    z, x = f // RING, f % RING
    xp, xm, x2 = (x + 1) % RING, (x + RING - 1) % RING, (x + 2) % RING
    zo = 1 - z
    fz, fxp, fxm = zo * RING + x, z * RING + xp, z * RING + xm
    ahead, behind, mirror = (s + 1) % sections, (s + sections - 1) % sections, sections - 1 - s
    core = s % 2
    sibling = s + 1 - 2 * core
    is_enc = s < sections // 2
    enc = jnp.where(is_enc, 1, 0)
    first = core == enc
    enc_f = enc.astype(F32)
    far_z = jnp.where(z == (s // min(8, sections)) % 2, 0, 1)
    forward_first = enc * far_z

    period = min(8, sections)
    place, run = s % period, s // period
    enc_before = jnp.where((s + sections - 1) % sections < sections // 2, 1, 0)
    enc_after = jnp.where((s + 1) % sections < sections // 2, 1, 0)
    far_f, far_b = place == period - 1, place == 0
    near_f, near_b = jnp.logical_not(far_f), jnp.logical_not(far_b)
    relay_f_at, relay_b_at = run * period + enc, run * period + period - 2 + enc
    is_relay_f, is_relay_b = s == relay_f_at, s == relay_b_at
    relay_f_from, relay_b_from = run * period + period - 1, run * period
    relay_f_to, relay_b_to = (run * period + period) % sections, (run * period + sections - 1) % sections
    relay_f_into = (run * period + sections - period) % sections + enc_before
    relay_b_into = (run * period + period) % sections + period - 2 + enc_after

    def at(section, fsdp):
        return {"section": section, "fsdp": fsdp}

    def remote(src, dst, send, recv, section, fsdp):
        return pltpu.make_async_remote_copy(
            src_ref=src, dst_ref=dst, send_sem=send, recv_sem=recv,
            device_id=at(section, fsdp), device_id_type=MESH,
        )

    fwpad[...] = jnp.zeros_like(fwpad)
    loads = [
        pltpu.make_async_copy(fw_in.at[0], fwpad.at[pl.ds(f * fws, fws)], load_sem.at[0]),
        pltpu.make_async_copy(stash.at[0], stash_v, load_sem.at[1]),
        pltpu.make_async_copy(held.at[0], held_v, load_sem.at[2]),
        pltpu.make_async_copy(tw_in.at[0], tw.at[pl.ds(f * tws, tws)], load_sem.at[3]),
        pltpu.make_async_copy(pw_in.at[0], pw.at[pl.ds(f * pws, pws)], load_sem.at[4]),
        pltpu.make_async_copy(hid, hid_all.at[:, f], load_sem.at[5]),
    ]
    for load in loads:
        load.start()

    barrier = pltpu.get_barrier_semaphore()
    for section in (ahead, behind, mirror):
        pl.semaphore_signal(barrier, inc=1, device_id=at(section, f), device_id_type=MESH)
    for d in range(1, n_fsdp):
        pl.semaphore_signal(barrier, inc=1, device_id=at(s, (f + d) % n_fsdp), device_id_type=MESH)
    greet = [(is_relay_f, relay_f_from), (is_relay_b, relay_b_from), (far_b, relay_f_into), (far_f, relay_b_into)]
    for role, section in greet:
        pl.when(role)(
            functools.partial(
                pl.semaphore_signal, barrier, inc=1, device_id=at(section, f), device_id_type=MESH
            )
        )
    extra = sum(jnp.where(role, 1, 0) for role in (far_f, far_b, is_relay_f, is_relay_b))
    pl.semaphore_wait(barrier, 3 + n_fsdp - 1 + extra)

    hid_out = [
        remote(hid, hid_all.at[:, f], hid_send.at[d], hid_recv.at[d], s, (f + d) % n_fsdp)
        for d in range(1, n_fsdp)
    ]

    h0 = {tws: (tws // 2 + 15) // 16 * 16, pws: pws // 2 // 16 * 16}

    def ag_copies(i, src_own, full, n):
        lo, hi = h0[n], n - h0[n]

        def shard(index):
            return full.at[pl.ds(index * n, n)]

        def low(index):
            return full.at[pl.ds(index * n, lo)]

        def high(index):
            return full.at[pl.ds(index * n + lo, hi)]

        fo_p, fo_m = zo * RING + xp, zo * RING + xm
        f_2, fo_2 = z * RING + x2, zo * RING + x2
        plan = [
            (src_own.at[0], shard(f), shard(fz), fz),
            (src_own.at[0], shard(f), shard(fxm), fxp),
            (src_own.at[0], shard(f), shard(fxp), fxm),
            (shard(fz), shard(fz), shard(fo_m), fxp),
            (shard(fz), shard(fz), shard(fo_p), fxm),
            (low(fxm), low(fxm), low(f_2), fxp),
            (high(fxp), high(fxp), high(f_2), fxm),
            (low(fo_m), low(fo_m), low(fo_2), fxp),
            (high(fo_p), high(fo_p), high(fo_2), fxm),
        ]
        sends, recvs = [], []
        for k, (src, dst, land, target) in enumerate(plan):
            sends.append(remote(src, dst, ag_send.at[i, k], ag_recv.at[i, k], s, target))
            recvs.append(remote(land, land, ag_send.at[i, k], ag_recv.at[i, k], s, target))
        return sends, recvs

    tw_sends, tw_recvs = ag_copies(0, tw_in, tw, tws)
    pw_sends, pw_recvs = ag_copies(1, pw_in, pw, pws)

    def start(pairs, ks):
        for k in ks:
            for sends in pairs:
                sends[k].start()

    both = (tw_sends, pw_sends)
    later = jnp.logical_not(first)

    @pl.when(first)
    def _():
        start(both, (0,))
        start(both, (1, 2))

    for copy in hid_out:
        copy.start()

    upper, lower = pl.ds(0, rows // 2), pl.ds(rows // 2, rows // 2)
    move_fa = remote(handoff.at[0, upper], arrived.at[upper], move_send.at[0], move_recv.at[0], ahead, f)
    move_fb = remote(handoff.at[0, lower], arrived.at[lower], move_send.at[1], move_recv.at[1], ahead, f)
    move_fr = remote(handoff.at[0, lower], relay_h, move_send.at[1], relay_recv.at[0], relay_f_at, f)
    pass_f = remote(relay_h, arrived.at[lower], relay_send.at[0], move_recv.at[1], relay_f_to, f)
    move_ba = remote(returning.at[0, upper], back.at[upper], move_send.at[2], move_recv.at[2], behind, f)
    move_bb = remote(returning.at[0, lower], back.at[lower], move_send.at[3], move_recv.at[3], behind, f)
    move_br = remote(returning.at[0, lower], relay_r, move_send.at[3], relay_recv.at[1], relay_b_at, f)
    pass_b = remote(relay_r, back.at[lower], relay_send.at[1], move_recv.at[3], relay_b_to, f)

    @pl.when(near_f)
    def _():
        move_fa.start()
        move_fb.start()

    @pl.when(near_b)
    def _():
        move_ba.start()
        move_bb.start()

    pl.when(far_f)(move_fr.start)
    pl.when(far_b)(move_br.start)

    for padded in (modf, modb, dtp):
        padded[0:cell] = jnp.zeros((cell, ch), BF16)
        padded[cell + rows : 2 * cell + rows] = jnp.zeros((cell, ch), BF16)

    loads[0].wait()
    loads[5].wait()
    for d in range(1, n_fsdp):
        came = (f + n_fsdp - d) % n_fsdp
        remote(hid, hid_all.at[:, came], hid_send.at[d], hid_recv.at[d], s, came).wait_recv()
    hidden = jnp.concatenate(
        [hid_all[r, j] for r in range(2) for j in range(n_fsdp)], axis=0
    ).astype(BF16)
    partial = dot(hidden, fwpad[...])
    for r in range(2):
        for j in range(n_fsdp):
            k = r * n_fsdp + j
            part[j, r] = partial[k : k + 1]
    part_out = []
    for d in range(1, n_fsdp):
        j = (f + d) % n_fsdp
        part_out.append(remote(part.at[j], film_in.at[f], part_send.at[d], part_recv.at[d], s, j))
    for copy in part_out:
        copy.start()

    @pl.when(later)
    def _():
        start(both, (0,))

    for recvs, sends in ((tw_recvs, tw_sends), (pw_recvs, pw_sends)):
        recvs[0].wait_recv()
        pl.when(first)(functools.partial(start, (sends,), (3, 4)))
    pl.when(far_f)(move_fa.start)
    pl.when(far_b)(move_ba.start)
    def scale_shift(r):
        return 1.0 + film[r, :, 0:ch], film[r, :, ch : 2 * ch]

    def modulate(read, r, dst):
        scale, shift = scale_shift(r)

        def step(i, carry):
            at_row = pl.multiple_of(i * small, small)
            v = read(at_row, small)
            rstd = lax.rsqrt(jnp.mean(v * v, axis=-1, keepdims=True) + EPS)
            dst[pl.ds(at_row + cell, small)] = (v * rstd * scale + shift).astype(BF16)
            return carry

        lax.fori_loop(0, rows // small, step, 0)

    def read_stash(r0, n):
        return stash_v[pl.ds(r0, n)].astype(F32)

    def read_forward(r0, n):
        return arrived[pl.ds(r0, n)].astype(F32) + held_v[pl.ds(r0, n)].astype(F32) * (1.0 - enc_f)

    def read_grad(r0, n):
        return back[pl.ds(r0, n)].astype(F32) + held_v[pl.ds(r0, n)].astype(F32) * enc_f

    def settle_film():
        for d in range(1, n_fsdp):
            came = (f + n_fsdp - d) % n_fsdp
            remote(part.at[came], film_in.at[came], part_send.at[d], part_recv.at[d], s, came).wait_recv()
        film_in[f] = part[f]
        film[...] = jnp.sum(film_in[...], axis=0)
        loads[1].wait()
        loads[2].wait()
        modulate(read_stash, 1, modb)

    @pl.when(later)
    def _():
        settle_film()
        pl.semaphore_wait(go, 1)
        for sends in both:
            start((sends,), (1, 2, 3, 4))

    for recvs, sends in ((tw_recvs, tw_sends), (pw_recvs, pw_sends)):
        recvs[1].wait_recv()
        sends[5].start()
        recvs[2].wait_recv()
        sends[6].start()
    @pl.when(is_relay_f)
    def _():
        move_fr.wait_recv()
        pass_f.start()

    @pl.when(is_relay_b)
    def _():
        move_br.wait_recv()
        pass_b.start()

    for recvs, sends in ((tw_recvs, tw_sends), (pw_recvs, pw_sends)):
        recvs[3].wait_recv()
        sends[7].start()
        recvs[4].wait_recv()
        sends[8].start()

    @pl.when(first)
    def _():
        pl.semaphore_signal(go, inc=1, device_id=at(sibling, f), device_id_type=MESH)
        settle_film()

    loads[3].wait()
    loads[4].wait()

    def gather_end(recvs):
        for k in range(5, 9):
            recvs[k].wait_recv()

    def skip_copy(src, c):
        piece = pl.ds(pl.multiple_of(c * chunk, chunk), chunk)
        return remote(src.at[piece], out_skip.at[0, piece], skip_send.at[c], skip_recv.at[c], mirror, f)

    def temporal_of(mod, r0):
        taps = [mod[pl.ds(pl.multiple_of(r0 + k * cell, cell), chunk)] for k in range(3)]
        return dot(jnp.concatenate(taps, axis=1), tw[...])

    out_f_copy = pltpu.make_async_copy(fout, out_f.at[0], out_sem.at[0])
    out_b_copy = pltpu.make_async_copy(bout, out_b.at[0], out_sem.at[1])

    def forward():
        move_fa.wait_recv()
        move_fb.wait_recv()
        modulate(read_forward, 0, modf)
        pl.when(forward_first == 1)(functools.partial(gather_end, tw_recvs))

        def step(c, carry):
            r0 = pl.multiple_of(c * chunk, chunk)
            t = temporal_of(modf, r0)
            gate = (t * sigmoid(t)).astype(BF16)
            pl.when(jnp.logical_and(c == 0, forward_first == 1))(functools.partial(gather_end, pw_recvs))
            fout[pl.ds(r0, chunk)] = (read_forward(r0, chunk) + dot(gate, pw[...])).astype(BF16)

            @pl.when(is_enc)
            def _():
                skip_copy(fout, c).start()

            return carry

        lax.fori_loop(0, rows // chunk, step, 0)
        out_f_copy.start()

    half = (tws + pws) // 2
    lo, hi = pl.ds(0, half), pl.ds(half, half)
    rs_plan = []
    for zi in (zo, z):
        rs_plan += [
            (grad.at[zi, x2, lo], ra_p.at[zi], fxp, fxm),
            (grad.at[zi, x2, hi], ra_m.at[zi], fxm, fxp),
            (grad.at[zi, xp, hi], rb_p.at[zi, hi], fxp, fxm),
            (grad.at[zi, xm, lo], rb_m.at[zi, lo], fxm, fxp),
            (ra_p.at[zi], rb_p.at[zi, lo], fxp, fxm),
            (ra_m.at[zi], rb_m.at[zi, hi], fxm, fxp),
        ]
    rs_plan.append((zsend, zrecv, fz, fz))
    rs = [
        remote(src, dst, rs_send.at[k], rs_recv.at[k], s, target)
        for k, (src, dst, target, _) in enumerate(rs_plan)
    ]
    df_out = [
        remote(dfilm.at[f], dfilm.at[f], df_send.at[d], df_recv.at[d], s, (f + d) % n_fsdp)
        for d in range(1, n_fsdp)
    ]

    def backward():
        move_ba.wait_recv()
        move_bb.wait_recv()
        pl.when(forward_first == 0)(functools.partial(gather_end, tw_recvs))
        sums[...] = jnp.zeros_like(sums)
        scale, _ = scale_shift(1)

        def step(c, carry):
            @pl.when(c < rows // chunk)
            def _():
                r0 = pl.multiple_of(c * chunk, chunk)
                t = temporal_of(modb, r0)
                sig = sigmoid(t)
                gated[pl.ds(r0, chunk)] = (t * sig).astype(BF16)
                g = read_grad(r0, chunk).astype(BF16)
                gb[pl.ds(r0, chunk)] = g
                pl.when(jnp.logical_and(c == 0, forward_first == 0))(functools.partial(gather_end, pw_recvs))
                dgate = nt(g, pw[...]).astype(BF16).astype(F32)
                dtp[pl.ds(pl.multiple_of(r0 + cell, cell), chunk)] = (
                    dgate * (sig * (1.0 + t * (1.0 - sig)))
                ).astype(BF16)

            @pl.when(c >= 1)
            def _():
                r0 = pl.multiple_of((c - 1) * chunk, chunk)
                dmod = jnp.zeros((chunk, ch), F32)
                for k in range(3):
                    piece = dtp[pl.ds(pl.multiple_of(r0 + (2 - k) * cell, cell), chunk)]
                    dmod += nt(piece, tw[k * ch : (k + 1) * ch])
                v = read_stash(r0, chunk)
                rstd = lax.rsqrt(jnp.mean(v * v, axis=-1, keepdims=True) + EPS)
                normalized = v * rstd
                sums[0] += jnp.sum((dmod * normalized).reshape(chunk // 8, 8, ch), axis=0)
                sums[1] += jnp.sum(dmod.reshape(chunk // 8, 8, ch), axis=0)
                dn = dmod * scale
                along = jnp.mean(dn * normalized, axis=-1, keepdims=True)
                bout[pl.ds(r0, chunk)] = (
                    read_grad(r0, chunk) + rstd * (dn - normalized * along)
                ).astype(BF16)

                @pl.when(jnp.logical_not(is_enc))
                def _():
                    skip_copy(bout, c - 1).start()

            return carry

        lax.fori_loop(0, rows // chunk + 1, step, 0)
        out_b_copy.start()
        dfilm[f] = jnp.concatenate(
            [jnp.sum(sums[0], axis=0, keepdims=True), jnp.sum(sums[1], axis=0, keepdims=True)], axis=1
        )
        for copy in df_out:
            copy.start()

        def turn(i, carry):
            cols = pl.ds(pl.multiple_of(i * 128, 128), 128)
            mod_t[cols] = modb[pl.ds(cell, rows), cols].T
            gated_t[cols] = gated[:, cols].T
            return carry

        lax.fori_loop(0, ch // 128, turn, 0)
        block = ch // 8
        for part_no in range(2):
            mrows = slice(part_no * ch // 2, (part_no + 1) * ch // 2)
            value = dot(gated_t[mrows], gb[...]).astype(BF16)
            for i in range(4):
                b = part_no * 4 + i
                grad[b // RING, b % RING, tws : tws + pws] = value[i * block : (i + 1) * block]
            for k in range(3):
                value = dot(mod_t[mrows], dtp[(2 - k) * cell : (2 - k) * cell + rows]).astype(BF16)
                for i in range(4):
                    b = k * 8 + part_no * 4 + i
                    j = b // 3
                    grad[j // RING, j % RING, (b % 3) * block : (b % 3 + 1) * block] = value[
                        i * block : (i + 1) * block
                    ]
        for k in (0, 1, 2, 3, 6, 7, 8, 9):
            rs[k].start()

    def phase(p, carry):
        which = p + forward_first
        pl.when(which == 1)(forward)
        pl.when(which != 1)(backward)
        return carry

    lax.fori_loop(0, 2, phase, 0)

    def add_on(dst, src):
        dst[...] = (dst[...].astype(F32) + src[...].astype(F32)).astype(BF16)

    for k, zi in ((0, zo), (6, z)):
        rs[k].wait_recv()
        add_on(ra_p.at[zi], grad.at[zi, xp, lo])
        rs[k + 4].start()
        rs[k + 1].wait_recv()
        add_on(ra_m.at[zi], grad.at[zi, xm, hi])
        rs[k + 5].start()

    for d in range(1, n_fsdp):
        came = (f + n_fsdp - d) % n_fsdp
        remote(dfilm.at[came], dfilm.at[came], df_send.at[d], df_recv.at[d], s, came).wait_recv()
    hidden_b = jnp.concatenate([hid_all[1, j] for j in range(n_fsdp)], axis=0).astype(BF16)
    dfilm_all = jnp.concatenate([dfilm[j] for j in range(n_fsdp)], axis=0).astype(BF16)
    fg[...] = lax.dot_general(hidden_b, dfilm_all, (((0,), (0,)), ((), ())), preferred_element_type=F32)
    fg_copy = pltpu.make_async_copy(fg.at[pl.ds(f * fws, fws)], out_fg.at[0], out_sem.at[2])
    fg_copy.start()

    def along_x(zi):
        return grad[zi, x].astype(F32) + rb_p[zi].astype(F32) + rb_m[zi].astype(F32)

    for k in range(2, 6):
        rs[k].wait_recv()
    zsend[...] = along_x(zo).astype(BF16)
    rs[12].start()
    for k in range(8, 12):
        rs[k].wait_recv()
    own = along_x(z)
    tg[...] = own[0:tws]
    pg[...] = own[tws : tws + pws]
    rs[12].wait_recv()
    tg[...] += zrecv[0:tws].astype(F32)
    pg[...] += zrecv[tws : tws + pws].astype(F32)
    tg_copy = pltpu.make_async_copy(tg, out_tg.at[0], out_sem.at[3])
    pg_copy = pltpu.make_async_copy(pg, out_pg.at[0], out_sem.at[4])
    tg_copy.start()
    pg_copy.start()

    for copy in hid_out + part_out + df_out + tw_sends + pw_sends + rs + [move_fa, move_fb, move_ba, move_bb]:
        copy.wait_send()
    pl.when(is_relay_f)(pass_f.wait_send)
    pl.when(is_relay_b)(pass_b.wait_send)

    def skip_end(c, carry):
        copy = skip_copy(fout, c)
        copy.wait_send()
        copy.wait_recv()
        return carry

    lax.fori_loop(0, rows // chunk, skip_end, 0)
    for copy in (out_f_copy, out_b_copy, fg_copy, tg_copy, pg_copy):
        copy.wait()


def settle(*refs):
    sources, results, held, sem_in, sem_out = refs[:6], refs[6:12], refs[12:18], refs[18], refs[19]
    pieces = []
    for k in range(6):
        count = 4 if k < 3 else 1
        n = sources[k].shape[1] // count
        pieces += [(k, pl.ds(i * n, n)) for i in range(count)]
    loads = [
        pltpu.make_async_copy(sources[k].at[:, piece], held[k].at[:, piece], sem_in.at[i])
        for i, (k, piece) in enumerate(pieces)
    ]
    stores = [
        pltpu.make_async_copy(held[k].at[:, piece], results[k].at[:, piece], sem_out.at[i])
        for i, (k, piece) in enumerate(pieces)
    ]
    for load in loads:
        load.start()
    for load, store in zip(loads, stores):
        load.wait()
        store.start()
    for store in stores:
        store.wait()


def body(
    handoff,
    returning,
    stashed_input,
    skip_held,
    timesteps_forward,
    timesteps_backward,
    section_level,
    level_embed,
    temporal_weight,
    point_weight,
    film_weight,
):
    sections, n_fsdp = lax.axis_size("section"), lax.axis_size("fsdp")
    _, rows, ch = handoff.shape
    tws, pws, fws = temporal_weight.shape[1], point_weight.shape[1], film_weight.shape[1]
    embed = level_embed.shape[1]
    cell = rows // FRAMES
    level_row = lookup_level(level_embed, section_level[0])
    steps = jnp.concatenate([timesteps_forward[0], timesteps_backward[0]])
    hid = time_hidden(steps, level_row).astype(F32)[:, None, :]

    def vmem(shape, dtype=BF16):
        return pltpu.VMEM(shape, dtype)

    act, padded = (rows, ch), (rows + 2 * cell, ch)
    shard, half = (tws + pws, ch), ((tws + pws) // 2, ch)
    dma = pltpu.SemaphoreType.DMA
    scratch = [
        vmem(act), vmem(act), vmem(act), vmem(act),
        vmem((tws * n_fsdp, ch)), vmem((pws * n_fsdp, ch)), vmem((embed, 2 * ch)),
        vmem((2, n_fsdp, 1, embed), F32),
        vmem((n_fsdp, 2, 1, 2 * ch), F32), vmem((n_fsdp, 2, 1, 2 * ch), F32), vmem((2, 1, 2 * ch), F32),
        vmem(padded), vmem(padded), vmem(padded),
        vmem(act), vmem(act), vmem(act), vmem(act),
        vmem((ch, rows)), vmem((ch, rows)),
        vmem((2, RING) + shard),
        vmem((2,) + half), vmem((2,) + half), vmem((2,) + shard), vmem((2,) + shard),
        vmem(shard), vmem(shard),
        vmem((2, 8, ch), F32), vmem((n_fsdp, 1, 2 * ch), F32),
        vmem((embed, 2 * ch), F32), vmem((tws, ch), F32), vmem((pws, ch), F32),
        vmem((rows // 2, ch)), vmem((rows // 2, ch)),
        dma((6,)), dma((4,)), dma((4,)), dma((n_fsdp,)), dma((n_fsdp,)), dma((n_fsdp,)), dma((n_fsdp,)),
        dma((n_fsdp,)), dma((n_fsdp,)), dma((2, 9)), dma((2, 9)), dma((8,)), dma((8,)), dma((13,)), dma((13,)),
        dma((5,)), dma((2,)), dma((2,)), pltpu.SemaphoreType.REGULAR,
    ]
    hbm = pl.BlockSpec(memory_space=pl.ANY)
    local = pl.BlockSpec(memory_space=pltpu.VMEM)
    like = jax.ShapeDtypeStruct
    shapes = (
        like(handoff.shape, BF16),
        like(handoff.shape, BF16),
        like(handoff.shape, BF16),
        like(temporal_weight.shape, F32),
        like(point_weight.shape, F32),
        like(film_weight.shape, F32),
    )
    made = pl.pallas_call(
        functools.partial(tick, sections),
        out_shape=shapes,
        in_specs=[local] + [hbm] * 7,
        out_specs=(hbm,) * 6,
        scratch_shapes=scratch,
        compiler_params=pltpu.CompilerParams(
            collective_id=0, has_side_effects=True, vmem_limit_bytes=56 * 1024 * 1024
        ),
        name="relay_tick",
    )(hid, handoff, returning, stashed_input, skip_held, temporal_weight, point_weight, film_weight)
    return tuple(
        pl.pallas_call(
            settle,
            out_shape=shapes,
            in_specs=[hbm] * 6,
            out_specs=(hbm,) * 6,
            scratch_shapes=[vmem(out.shape, out.dtype) for out in shapes] + [dma((15,)), dma((15,))],
            compiler_params=pltpu.CompilerParams(vmem_limit_bytes=60 * 1024 * 1024),
            name="settle",
        )(*made)
    )


def solution(mesh):
    rows = P("section", "fsdp", None)
    in_specs = (rows, rows, rows, rows, P("section", "fsdp"), P("section", "fsdp"), P("section"), P(), rows, rows, rows)
    return jax.shard_map(body, mesh=mesh, in_specs=in_specs, out_specs=(rows,) * 6, check_vma=False)
```

```python
import functools
import math

import jax
import jax.numpy as jnp
from jax import lax
from jax.experimental import pallas as pl
from jax.experimental.pallas import tpu as pltpu
from jax.sharding import PartitionSpec as P

FRAMES = 16
LEVELS = 4
RING = 4
EPS = 1e-06
F32 = jnp.float32
BF16 = jnp.bfloat16
MESH = pl.DeviceIdType.MESH


def lookup_level(level_embed, level_index):
    onehot = (jnp.arange(LEVELS, dtype=jnp.int32) == level_index).astype(F32)
    return jnp.sum(onehot[:, None] * level_embed, axis=0)


def time_hidden(timesteps, level_row):
    half_width = level_row.shape[0] // 2
    frequency = jnp.exp(-math.log(10000.0) * jnp.arange(half_width, dtype=F32) / half_width)
    phases = timesteps.astype(F32)[:, None] * frequency[None, :]
    embedded = jnp.concatenate([jnp.sin(phases), jnp.cos(phases)], axis=-1) + level_row[None, :]
    return jax.nn.silu(embedded).astype(BF16)


def sigmoid(t):
    return 0.5 + 0.5 * jnp.tanh(0.5 * t)


def nt(a, b):
    return lax.dot_general(a, b, (((1,), (1,)), ((), ())), preferred_element_type=F32)


def dot(a, b):
    return jnp.dot(a, b, preferred_element_type=F32)


def tick(
    sections,
    hid, handoff, returning, stash, held, tw_in, pw_in, fw_in,
    out_f, out_b, out_skip, out_tg, out_pg, out_fg,
    arrived, back, stash_v, held_v, tw, pw, fwpad, hid_all, part, film_in, film,
    modf, modb, dtp, gated, gb, fout, bout, mod_t, gated_t, grad,
    ra_p, ra_m, rb_p, rb_m, zsend, zrecv, sums, dfilm, fg, tg, pg, relay_h, relay_r,
    load_sem, move_send, move_recv, hid_send, hid_recv, part_send, part_recv,
    df_send, df_recv, ag_send, ag_recv, skip_send, skip_recv, rs_send, rs_recv, out_sem,
    relay_send, relay_recv, go,
):
    rows, ch = arrived.shape
    cell = rows // FRAMES
    chunk = rows // 8
    small = cell
    tws, pws, fws = tw_in.shape[1], pw_in.shape[1], fw_in.shape[1]
    n_fsdp = 2 * RING
    s, f = lax.axis_index("section"), lax.axis_index("fsdp")
    z, x = f // RING, f % RING
    xp, xm, x2 = (x + 1) % RING, (x + RING - 1) % RING, (x + 2) % RING
    zo = 1 - z
    fz, fxp, fxm = zo * RING + x, z * RING + xp, z * RING + xm
    ahead, behind, mirror = (s + 1) % sections, (s + sections - 1) % sections, sections - 1 - s
    core = s % 2
    sibling = s + 1 - 2 * core
    is_enc = s < sections // 2
    enc = jnp.where(is_enc, 1, 0)
    first = core == enc
    enc_f = enc.astype(F32)
    far_z = jnp.where(z == (s // min(8, sections)) % 2, 0, 1)
    forward_first = enc * far_z * jnp.where(first, 1, 0)

    period = min(8, sections)
    place, run = s % period, s // period
    enc_before = jnp.where((s + sections - 1) % sections < sections // 2, 1, 0)
    enc_after = jnp.where((s + 1) % sections < sections // 2, 1, 0)
    far_f, far_b = place == period - 1, place == 0
    near_f, near_b = jnp.logical_not(far_f), jnp.logical_not(far_b)
    relay_f_at, relay_b_at = run * period + enc, run * period + period - 2 + enc
    is_relay_f, is_relay_b = s == relay_f_at, s == relay_b_at
    relay_f_from, relay_b_from = run * period + period - 1, run * period
    relay_f_to, relay_b_to = (run * period + period) % sections, (run * period + sections - 1) % sections
    relay_f_into = (run * period + sections - period) % sections + enc_before
    relay_b_into = (run * period + period) % sections + period - 2 + enc_after

    def at(section, fsdp):
        return {"section": section, "fsdp": fsdp}

    def remote(src, dst, send, recv, section, fsdp):
        return pltpu.make_async_remote_copy(
            src_ref=src, dst_ref=dst, send_sem=send, recv_sem=recv,
            device_id=at(section, fsdp), device_id_type=MESH,
        )

    fwpad[...] = jnp.zeros_like(fwpad)
    loads = [
        pltpu.make_async_copy(fw_in.at[0], fwpad.at[pl.ds(f * fws, fws)], load_sem.at[0]),
        pltpu.make_async_copy(stash.at[0], stash_v, load_sem.at[1]),
        pltpu.make_async_copy(held.at[0], held_v, load_sem.at[2]),
        pltpu.make_async_copy(tw_in.at[0], tw.at[pl.ds(f * tws, tws)], load_sem.at[3]),
        pltpu.make_async_copy(pw_in.at[0], pw.at[pl.ds(f * pws, pws)], load_sem.at[4]),
        pltpu.make_async_copy(hid, hid_all.at[:, f], load_sem.at[5]),
    ]
    for load in loads:
        load.start()

    barrier = pltpu.get_barrier_semaphore()
    for section in (ahead, behind, mirror):
        pl.semaphore_signal(barrier, inc=1, device_id=at(section, f), device_id_type=MESH)
    for d in range(1, n_fsdp):
        pl.semaphore_signal(barrier, inc=1, device_id=at(s, (f + d) % n_fsdp), device_id_type=MESH)
    greet = [(is_relay_f, relay_f_from), (is_relay_b, relay_b_from), (far_b, relay_f_into), (far_f, relay_b_into)]
    for role, section in greet:
        pl.when(role)(
            functools.partial(
                pl.semaphore_signal, barrier, inc=1, device_id=at(section, f), device_id_type=MESH
            )
        )
    extra = sum(jnp.where(role, 1, 0) for role in (far_f, far_b, is_relay_f, is_relay_b))
    pl.semaphore_wait(barrier, 3 + n_fsdp - 1 + extra)

    hid_out = [
        remote(hid, hid_all.at[:, f], hid_send.at[d], hid_recv.at[d], s, (f + d) % n_fsdp)
        for d in range(1, n_fsdp)
    ]

    h0 = {tws: (tws // 2 + 15) // 16 * 16, pws: pws // 2 // 16 * 16}

    def ag_copies(i, src_own, full, n):
        lo, hi = h0[n], n - h0[n]

        def shard(index):
            return full.at[pl.ds(index * n, n)]

        def low(index):
            return full.at[pl.ds(index * n, lo)]

        def high(index):
            return full.at[pl.ds(index * n + lo, hi)]

        fo_p, fo_m = zo * RING + xp, zo * RING + xm
        f_2, fo_2 = z * RING + x2, zo * RING + x2
        plan = [
            (src_own.at[0], shard(f), shard(fz), fz),
            (src_own.at[0], shard(f), shard(fxm), fxp),
            (src_own.at[0], shard(f), shard(fxp), fxm),
            (shard(fz), shard(fz), shard(fo_m), fxp),
            (shard(fz), shard(fz), shard(fo_p), fxm),
            (low(fxm), low(fxm), low(f_2), fxp),
            (high(fxp), high(fxp), high(f_2), fxm),
            (low(fo_m), low(fo_m), low(fo_2), fxp),
            (high(fo_p), high(fo_p), high(fo_2), fxm),
        ]
        sends, recvs = [], []
        for k, (src, dst, land, target) in enumerate(plan):
            sends.append(remote(src, dst, ag_send.at[i, k], ag_recv.at[i, k], s, target))
            recvs.append(remote(land, land, ag_send.at[i, k], ag_recv.at[i, k], s, target))
        return sends, recvs

    tw_sends, tw_recvs = ag_copies(0, tw_in, tw, tws)
    pw_sends, pw_recvs = ag_copies(1, pw_in, pw, pws)

    def start(pairs, ks):
        for k in ks:
            for sends in pairs:
                sends[k].start()

    both = (tw_sends, pw_sends)
    later = jnp.logical_not(first)

    @pl.when(first)
    def _():
        start(both, (0,))
        start(both, (1, 2))

    for copy in hid_out:
        copy.start()

    upper, lower = pl.ds(0, rows // 2), pl.ds(rows // 2, rows // 2)
    move_fa = remote(handoff.at[0, upper], arrived.at[upper], move_send.at[0], move_recv.at[0], ahead, f)
    move_fb = remote(handoff.at[0, lower], arrived.at[lower], move_send.at[1], move_recv.at[1], ahead, f)
    move_fr = remote(handoff.at[0, lower], relay_h, move_send.at[1], relay_recv.at[0], relay_f_at, f)
    pass_f = remote(relay_h, arrived.at[lower], relay_send.at[0], move_recv.at[1], relay_f_to, f)
    move_ba = remote(returning.at[0, upper], back.at[upper], move_send.at[2], move_recv.at[2], behind, f)
    move_bb = remote(returning.at[0, lower], back.at[lower], move_send.at[3], move_recv.at[3], behind, f)
    move_br = remote(returning.at[0, lower], relay_r, move_send.at[3], relay_recv.at[1], relay_b_at, f)
    pass_b = remote(relay_r, back.at[lower], relay_send.at[1], move_recv.at[3], relay_b_to, f)

    @pl.when(near_f)
    def _():
        move_fa.start()
        move_fb.start()

    @pl.when(near_b)
    def _():
        move_ba.start()
        move_bb.start()

    pl.when(far_f)(move_fr.start)
    pl.when(far_b)(move_br.start)

    for padded in (modf, modb, dtp):
        padded[0:cell] = jnp.zeros((cell, ch), BF16)
        padded[cell + rows : 2 * cell + rows] = jnp.zeros((cell, ch), BF16)

    loads[0].wait()
    loads[5].wait()
    for d in range(1, n_fsdp):
        came = (f + n_fsdp - d) % n_fsdp
        remote(hid, hid_all.at[:, came], hid_send.at[d], hid_recv.at[d], s, came).wait_recv()
    hidden = jnp.concatenate(
        [hid_all[r, j] for r in range(2) for j in range(n_fsdp)], axis=0
    ).astype(BF16)
    partial = dot(hidden, fwpad[...])
    for r in range(2):
        for j in range(n_fsdp):
            k = r * n_fsdp + j
            part[j, r] = partial[k : k + 1]
    part_out = []
    for d in range(1, n_fsdp):
        j = (f + d) % n_fsdp
        part_out.append(remote(part.at[j], film_in.at[f], part_send.at[d], part_recv.at[d], s, j))
    for copy in part_out:
        copy.start()

    @pl.when(later)
    def _():
        start(both, (0,))

    for recvs, sends in ((tw_recvs, tw_sends), (pw_recvs, pw_sends)):
        recvs[0].wait_recv()
        pl.when(first)(functools.partial(start, (sends,), (3, 4)))
    pl.when(far_f)(move_fa.start)
    pl.when(far_b)(move_ba.start)
    def scale_shift(r):
        return 1.0 + film[r, :, 0:ch], film[r, :, ch : 2 * ch]

    def modulate(read, r, dst):
        scale, shift = scale_shift(r)

        def step(i, carry):
            at_row = pl.multiple_of(i * small, small)
            v = read(at_row, small)
            rstd = lax.rsqrt(jnp.mean(v * v, axis=-1, keepdims=True) + EPS)
            dst[pl.ds(at_row + cell, small)] = (v * rstd * scale + shift).astype(BF16)
            return carry

        lax.fori_loop(0, rows // small, step, 0)

    def read_stash(r0, n):
        return stash_v[pl.ds(r0, n)].astype(F32)

    def read_forward(r0, n):
        return arrived[pl.ds(r0, n)].astype(F32) + held_v[pl.ds(r0, n)].astype(F32) * (1.0 - enc_f)

    def read_grad(r0, n):
        return back[pl.ds(r0, n)].astype(F32) + held_v[pl.ds(r0, n)].astype(F32) * enc_f

    def settle_film():
        for d in range(1, n_fsdp):
            came = (f + n_fsdp - d) % n_fsdp
            remote(part.at[came], film_in.at[came], part_send.at[d], part_recv.at[d], s, came).wait_recv()
        film_in[f] = part[f]
        film[...] = jnp.sum(film_in[...], axis=0)
        loads[1].wait()
        loads[2].wait()
        modulate(read_stash, 1, modb)

    @pl.when(later)
    def _():
        settle_film()
        pl.semaphore_wait(go, 1)
        for sends in both:
            start((sends,), (1, 2, 3, 4))

    for recvs, sends in ((tw_recvs, tw_sends), (pw_recvs, pw_sends)):
        recvs[1].wait_recv()
        sends[5].start()
        recvs[2].wait_recv()
        sends[6].start()
    @pl.when(is_relay_f)
    def _():
        move_fr.wait_recv()
        pass_f.start()

    @pl.when(is_relay_b)
    def _():
        move_br.wait_recv()
        pass_b.start()

    for recvs, sends in ((tw_recvs, tw_sends), (pw_recvs, pw_sends)):
        recvs[3].wait_recv()
        sends[7].start()
        recvs[4].wait_recv()
        sends[8].start()

    @pl.when(first)
    def _():
        pl.semaphore_signal(go, inc=1, device_id=at(sibling, f), device_id_type=MESH)
        settle_film()

    loads[3].wait()
    loads[4].wait()

    def gather_end(recvs):
        for k in range(5, 9):
            recvs[k].wait_recv()

    def skip_copy(src, c):
        piece = pl.ds(pl.multiple_of(c * chunk, chunk), chunk)
        return remote(src.at[piece], out_skip.at[0, piece], skip_send.at[c], skip_recv.at[c], mirror, f)

    def temporal_of(mod, r0):
        taps = [mod[pl.ds(pl.multiple_of(r0 + k * cell, cell), chunk)] for k in range(3)]
        return dot(jnp.concatenate(taps, axis=1), tw[...])

    out_f_copy = pltpu.make_async_copy(fout, out_f.at[0], out_sem.at[0])
    out_b_copy = pltpu.make_async_copy(bout, out_b.at[0], out_sem.at[1])

    def forward():
        move_fa.wait_recv()
        move_fb.wait_recv()
        modulate(read_forward, 0, modf)
        pl.when(forward_first == 1)(functools.partial(gather_end, tw_recvs))

        def step(c, carry):
            r0 = pl.multiple_of(c * chunk, chunk)
            t = temporal_of(modf, r0)
            gate = (t * sigmoid(t)).astype(BF16)
            pl.when(jnp.logical_and(c == 0, forward_first == 1))(functools.partial(gather_end, pw_recvs))
            fout[pl.ds(r0, chunk)] = (read_forward(r0, chunk) + dot(gate, pw[...])).astype(BF16)

            @pl.when(is_enc)
            def _():
                skip_copy(fout, c).start()

            return carry

        lax.fori_loop(0, rows // chunk, step, 0)
        out_f_copy.start()

    half = (tws + pws) // 2
    lo, hi = pl.ds(0, half), pl.ds(half, half)
    rs_plan = []
    for zi in (zo, z):
        rs_plan += [
            (grad.at[zi, x2, lo], ra_p.at[zi], fxp, fxm),
            (grad.at[zi, x2, hi], ra_m.at[zi], fxm, fxp),
            (grad.at[zi, xp, hi], rb_p.at[zi, hi], fxp, fxm),
            (grad.at[zi, xm, lo], rb_m.at[zi, lo], fxm, fxp),
            (ra_p.at[zi], rb_p.at[zi, lo], fxp, fxm),
            (ra_m.at[zi], rb_m.at[zi, hi], fxm, fxp),
        ]
    rs_plan.append((zsend, zrecv, fz, fz))
    rs = [
        remote(src, dst, rs_send.at[k], rs_recv.at[k], s, target)
        for k, (src, dst, target, _) in enumerate(rs_plan)
    ]
    df_out = [
        remote(dfilm.at[f], dfilm.at[f], df_send.at[d], df_recv.at[d], s, (f + d) % n_fsdp)
        for d in range(1, n_fsdp)
    ]

    def backward():
        move_ba.wait_recv()
        move_bb.wait_recv()
        pl.when(forward_first == 0)(functools.partial(gather_end, tw_recvs))
        sums[...] = jnp.zeros_like(sums)
        scale, _ = scale_shift(1)

        def step(c, carry):
            @pl.when(c < rows // chunk)
            def _():
                r0 = pl.multiple_of(c * chunk, chunk)
                t = temporal_of(modb, r0)
                sig = sigmoid(t)
                gated[pl.ds(r0, chunk)] = (t * sig).astype(BF16)
                g = read_grad(r0, chunk).astype(BF16)
                gb[pl.ds(r0, chunk)] = g
                pl.when(jnp.logical_and(c == 0, forward_first == 0))(functools.partial(gather_end, pw_recvs))
                dgate = nt(g, pw[...]).astype(BF16).astype(F32)
                dtp[pl.ds(pl.multiple_of(r0 + cell, cell), chunk)] = (
                    dgate * (sig * (1.0 + t * (1.0 - sig)))
                ).astype(BF16)

            @pl.when(c >= 1)
            def _():
                r0 = pl.multiple_of((c - 1) * chunk, chunk)
                dmod = jnp.zeros((chunk, ch), F32)
                for k in range(3):
                    piece = dtp[pl.ds(pl.multiple_of(r0 + (2 - k) * cell, cell), chunk)]
                    dmod += nt(piece, tw[k * ch : (k + 1) * ch])
                v = read_stash(r0, chunk)
                rstd = lax.rsqrt(jnp.mean(v * v, axis=-1, keepdims=True) + EPS)
                normalized = v * rstd
                sums[0] += jnp.sum((dmod * normalized).reshape(chunk // 8, 8, ch), axis=0)
                sums[1] += jnp.sum(dmod.reshape(chunk // 8, 8, ch), axis=0)
                dn = dmod * scale
                along = jnp.mean(dn * normalized, axis=-1, keepdims=True)
                bout[pl.ds(r0, chunk)] = (
                    read_grad(r0, chunk) + rstd * (dn - normalized * along)
                ).astype(BF16)

                @pl.when(jnp.logical_not(is_enc))
                def _():
                    skip_copy(bout, c - 1).start()

            return carry

        lax.fori_loop(0, rows // chunk + 1, step, 0)
        out_b_copy.start()
        dfilm[f] = jnp.concatenate(
            [jnp.sum(sums[0], axis=0, keepdims=True), jnp.sum(sums[1], axis=0, keepdims=True)], axis=1
        )
        for copy in df_out:
            copy.start()

        def turn(i, carry):
            cols = pl.ds(pl.multiple_of(i * 128, 128), 128)
            mod_t[cols] = modb[pl.ds(cell, rows), cols].T
            gated_t[cols] = gated[:, cols].T
            return carry

        lax.fori_loop(0, ch // 128, turn, 0)
        block = ch // 8
        for part_no in range(2):
            mrows = slice(part_no * ch // 2, (part_no + 1) * ch // 2)
            value = dot(gated_t[mrows], gb[...]).astype(BF16)
            for i in range(4):
                b = part_no * 4 + i
                grad[b // RING, b % RING, tws : tws + pws] = value[i * block : (i + 1) * block]
            for k in range(3):
                value = dot(mod_t[mrows], dtp[(2 - k) * cell : (2 - k) * cell + rows]).astype(BF16)
                for i in range(4):
                    b = k * 8 + part_no * 4 + i
                    j = b // 3
                    grad[j // RING, j % RING, (b % 3) * block : (b % 3 + 1) * block] = value[
                        i * block : (i + 1) * block
                    ]
        for k in (0, 1, 2, 3, 6, 7, 8, 9):
            rs[k].start()

    def phase(p, carry):
        which = p + forward_first
        pl.when(which == 1)(forward)
        pl.when(which != 1)(backward)
        return carry

    lax.fori_loop(0, 2, phase, 0)

    def add_on(dst, src):
        dst[...] = (dst[...].astype(F32) + src[...].astype(F32)).astype(BF16)

    for k, zi in ((0, zo), (6, z)):
        rs[k].wait_recv()
        add_on(ra_p.at[zi], grad.at[zi, xp, lo])
        rs[k + 4].start()
        rs[k + 1].wait_recv()
        add_on(ra_m.at[zi], grad.at[zi, xm, hi])
        rs[k + 5].start()

    for d in range(1, n_fsdp):
        came = (f + n_fsdp - d) % n_fsdp
        remote(dfilm.at[came], dfilm.at[came], df_send.at[d], df_recv.at[d], s, came).wait_recv()
    hidden_b = jnp.concatenate([hid_all[1, j] for j in range(n_fsdp)], axis=0).astype(BF16)
    dfilm_all = jnp.concatenate([dfilm[j] for j in range(n_fsdp)], axis=0).astype(BF16)
    fg[...] = lax.dot_general(hidden_b, dfilm_all, (((0,), (0,)), ((), ())), preferred_element_type=F32)
    fg_copy = pltpu.make_async_copy(fg.at[pl.ds(f * fws, fws)], out_fg.at[0], out_sem.at[2])
    fg_copy.start()

    def along_x(zi):
        return grad[zi, x].astype(F32) + rb_p[zi].astype(F32) + rb_m[zi].astype(F32)

    for k in range(2, 6):
        rs[k].wait_recv()
    zsend[...] = along_x(zo).astype(BF16)
    rs[12].start()
    for k in range(8, 12):
        rs[k].wait_recv()
    own = along_x(z)
    tg[...] = own[0:tws]
    pg[...] = own[tws : tws + pws]
    rs[12].wait_recv()
    tg[...] += zrecv[0:tws].astype(F32)
    pg[...] += zrecv[tws : tws + pws].astype(F32)
    tg_copy = pltpu.make_async_copy(tg, out_tg.at[0], out_sem.at[3])
    pg_copy = pltpu.make_async_copy(pg, out_pg.at[0], out_sem.at[4])
    tg_copy.start()
    pg_copy.start()

    for copy in hid_out + part_out + df_out + tw_sends + pw_sends + rs + [move_fa, move_fb, move_ba, move_bb]:
        copy.wait_send()
    pl.when(is_relay_f)(pass_f.wait_send)
    pl.when(is_relay_b)(pass_b.wait_send)

    def skip_end(c, carry):
        copy = skip_copy(fout, c)
        copy.wait_send()
        copy.wait_recv()
        return carry

    lax.fori_loop(0, rows // chunk, skip_end, 0)
    for copy in (out_f_copy, out_b_copy, fg_copy, tg_copy, pg_copy):
        copy.wait()


def settle(*refs):
    sources, results, held, sem_in, sem_out = refs[:6], refs[6:12], refs[12:18], refs[18], refs[19]
    pieces = []
    for k in range(6):
        count = 4 if k < 3 else 1
        n = sources[k].shape[1] // count
        pieces += [(k, pl.ds(i * n, n)) for i in range(count)]
    loads = [
        pltpu.make_async_copy(sources[k].at[:, piece], held[k].at[:, piece], sem_in.at[i])
        for i, (k, piece) in enumerate(pieces)
    ]
    stores = [
        pltpu.make_async_copy(held[k].at[:, piece], results[k].at[:, piece], sem_out.at[i])
        for i, (k, piece) in enumerate(pieces)
    ]
    for load in loads:
        load.start()
    for load, store in zip(loads, stores):
        load.wait()
        store.start()
    for store in stores:
        store.wait()


def body(
    handoff,
    returning,
    stashed_input,
    skip_held,
    timesteps_forward,
    timesteps_backward,
    section_level,
    level_embed,
    temporal_weight,
    point_weight,
    film_weight,
):
    sections, n_fsdp = lax.axis_size("section"), lax.axis_size("fsdp")
    _, rows, ch = handoff.shape
    tws, pws, fws = temporal_weight.shape[1], point_weight.shape[1], film_weight.shape[1]
    embed = level_embed.shape[1]
    cell = rows // FRAMES
    level_row = lookup_level(level_embed, section_level[0])
    steps = jnp.concatenate([timesteps_forward[0], timesteps_backward[0]])
    hid = time_hidden(steps, level_row).astype(F32)[:, None, :]

    def vmem(shape, dtype=BF16):
        return pltpu.VMEM(shape, dtype)

    act, padded = (rows, ch), (rows + 2 * cell, ch)
    shard, half = (tws + pws, ch), ((tws + pws) // 2, ch)
    dma = pltpu.SemaphoreType.DMA
    scratch = [
        vmem(act), vmem(act), vmem(act), vmem(act),
        vmem((tws * n_fsdp, ch)), vmem((pws * n_fsdp, ch)), vmem((embed, 2 * ch)),
        vmem((2, n_fsdp, 1, embed), F32),
        vmem((n_fsdp, 2, 1, 2 * ch), F32), vmem((n_fsdp, 2, 1, 2 * ch), F32), vmem((2, 1, 2 * ch), F32),
        vmem(padded), vmem(padded), vmem(padded),
        vmem(act), vmem(act), vmem(act), vmem(act),
        vmem((ch, rows)), vmem((ch, rows)),
        vmem((2, RING) + shard),
        vmem((2,) + half), vmem((2,) + half), vmem((2,) + shard), vmem((2,) + shard),
        vmem(shard), vmem(shard),
        vmem((2, 8, ch), F32), vmem((n_fsdp, 1, 2 * ch), F32),
        vmem((embed, 2 * ch), F32), vmem((tws, ch), F32), vmem((pws, ch), F32),
        vmem((rows // 2, ch)), vmem((rows // 2, ch)),
        dma((6,)), dma((4,)), dma((4,)), dma((n_fsdp,)), dma((n_fsdp,)), dma((n_fsdp,)), dma((n_fsdp,)),
        dma((n_fsdp,)), dma((n_fsdp,)), dma((2, 9)), dma((2, 9)), dma((8,)), dma((8,)), dma((13,)), dma((13,)),
        dma((5,)), dma((2,)), dma((2,)), pltpu.SemaphoreType.REGULAR,
    ]
    hbm = pl.BlockSpec(memory_space=pl.ANY)
    local = pl.BlockSpec(memory_space=pltpu.VMEM)
    like = jax.ShapeDtypeStruct
    shapes = (
        like(handoff.shape, BF16),
        like(handoff.shape, BF16),
        like(handoff.shape, BF16),
        like(temporal_weight.shape, F32),
        like(point_weight.shape, F32),
        like(film_weight.shape, F32),
    )
    made = pl.pallas_call(
        functools.partial(tick, sections),
        out_shape=shapes,
        in_specs=[local] + [hbm] * 7,
        out_specs=(hbm,) * 6,
        scratch_shapes=scratch,
        compiler_params=pltpu.CompilerParams(
            collective_id=0, has_side_effects=True, vmem_limit_bytes=56 * 1024 * 1024
        ),
        name="relay_tick",
    )(hid, handoff, returning, stashed_input, skip_held, temporal_weight, point_weight, film_weight)
    return tuple(
        pl.pallas_call(
            settle,
            out_shape=shapes,
            in_specs=[hbm] * 6,
            out_specs=(hbm,) * 6,
            scratch_shapes=[vmem(out.shape, out.dtype) for out in shapes] + [dma((15,)), dma((15,))],
            compiler_params=pltpu.CompilerParams(vmem_limit_bytes=60 * 1024 * 1024),
            name="settle",
        )(*made)
    )


def solution(mesh):
    rows = P("section", "fsdp", None)
    in_specs = (rows, rows, rows, rows, P("section", "fsdp"), P("section", "fsdp"), P("section"), P(), rows, rows, rows)
    return jax.shard_map(body, mesh=mesh, in_specs=in_specs, out_specs=(rows,) * 6, check_vma=False)
```
